128 devices in a mesh: dp: 16 (over x, y), ep: 8 (over z, core).
Axes of the slice: x: 4, y: 4, z: 4, core: 2. Of those that a mesh axis runs over, the one named last changes fastest.
Arguments:
- queries: bfloat16 [4096, 64, 576], P('dp', 'ep'), may hold values from -24 to 24
- prefix_latents: bfloat16 [16, 2048, 576], P('dp', 'ep'), may hold values from -6 to 6
- new_latents: bfloat16 [16, 256, 576], P('dp', 'ep'), may hold values from -6 to 6
- prefix_lengths: int32 [16], replicated, may hold values from 2 to 2048, as said below
- span_sources: int32 [16], replicated, may hold values from 0 to 15, as said below
- value_up: bfloat16 [64, 512, 128], P('ep'), may hold values from -0.25 to 0.25
- out_proj: bfloat16 [8192, 3584], P('ep', 'dp'), may hold values from -0.5 to 0.5
- residual: bfloat16 [4096, 3584], P(('dp', 'ep')), may hold values from -54 to 54
- norm_gain: bfloat16 [3584], replicated, may hold values from 0.099609375 to 1.8984375
- expert_gate: bfloat16 [128, 3584, 1024], P(('dp', 'ep')), may hold values from -0.09375 to 0.09375
- expert_up: bfloat16 [128, 3584, 1024], P(('dp', 'ep')), may hold values from -0.09375 to 0.09375
- expert_down: bfloat16 [128, 1024, 3584], P(('dp', 'ep')), may hold values from -0.1875 to 0.1875
- expert_ids: int32 [4096, 8], P(('dp', 'ep')), may hold values from 0 to 127, all different within a row; in each aligned block of 32 rows (0 to 31, 32 to 63, ...) at most 2 rows name the same one
- gate_weights: float32 [4096, 8], P(('dp', 'ep')), may hold values from 0.05 to 0.5
- decode_owner: int32 [16], replicated, may hold values from 0 to 15, each once
Outputs:
- layer_out: bfloat16 [4096, 3584], P(('dp', 'ep'))
- decode_latents: bfloat16 [16, 256, 576], P('dp', 'ep')
The draws below stay inside these ranges and needn't reach their ends.
Inputs may be any that keep to these rules, and one draw needn't show every extreme that they name: `prefix_lengths`: one prompt has all 2048 cached positions valid. `span_sources`: a permutation of the prompts. `expert_ids`: each row names 8 different experts; among the rows of one device (aligned blocks of 32 rows) no expert is named by more than 2 rows, and in some blocks one expert is named by exactly 2. `decode_owner`: a permutation of the prompts; slot o of decode_latents lives on index o of dp.
All inputs are finite; a program needn't handle non-finite values.
Results may differ from the reference program's by a relative error of at most 0.017.
Values may be sent and summed in bfloat16 or wider, within the bound.
A program may use at most 192 MiB of HBM per device.

```python
import math
import jax
import jax.numpy as jnp
import numpy as np
from jax import lax

D = 3584
HEADS = 64
LAT = 512
KVW = 576
VH = 128
MOE_FF = 1024
TOP = 8
EXPERTS = 128
SPAN = 256
LATE = 64
PREFIX = 2048
PROMPTS = 16
TOKENS = 4096
CAP = 2
N_DP = 16
N_EP = 8


def draw_queries(key, part):
    key = jax.random.fold_in(key, 3)
    values = jnp.clip(jax.random.normal(key, (TOKENS, HEADS, KVW), jnp.float32), -6.0, 6.0)
    return values.astype(jnp.bfloat16)


def draw_prefix_latents(key, part):
    key = jax.random.fold_in(key, 4)
    values = jnp.clip(jax.random.normal(key, (PROMPTS, PREFIX, KVW), jnp.float32), -6.0, 6.0)
    return values.astype(jnp.bfloat16)


def draw_residual(key, part):
    key = jax.random.fold_in(key, 5)
    subkeys = jax.random.split(key, 3)
    row_scale = jnp.exp(jax.random.uniform(subkeys[0], (TOKENS, 1), jnp.float32, math.log(0.3), math.log(3.0)))
    col_scale = jnp.exp(jax.random.uniform(subkeys[1], (1, D), jnp.float32, math.log(0.3), math.log(3.0)))
    base_values = jnp.clip(jax.random.normal(subkeys[2], (TOKENS, D), jnp.float32), -6.0, 6.0)
    return (base_values * row_scale * col_scale).astype(jnp.bfloat16)


def draw_prefix_lengths(key, part):
    key = jax.random.fold_in(key, 6)
    subkeys = jax.random.split(key, 2)
    lengths = jax.random.randint(subkeys[0], (PROMPTS,), 2, PREFIX + 1)
    longest = jax.random.randint(subkeys[1], (), 0, PROMPTS)
    return lengths.at[longest].set(PREFIX).astype(jnp.int32)


def draw_span_sources(key, part):
    key = jax.random.fold_in(key, 7)
    subkeys = jax.random.split(key, 2)
    order = jax.random.permutation(subkeys[0], PROMPTS).astype(jnp.int32)
    anchor = jax.random.randint(subkeys[1], (), 0, PROMPTS).astype(jnp.int32)
    partner = (anchor + PROMPTS // 2) % PROMPTS
    places = jnp.arange(PROMPTS, dtype=jnp.int32)
    holder = jnp.sum(jnp.where(order == partner, places, 0))
    displaced = jnp.sum(jnp.where(places == anchor, order, 0))
    order = jnp.where(places == holder, displaced, order)
    order = jnp.where(places == anchor, partner, order)
    return order.astype(jnp.int32)


def levels(stream_key, dims, cuts, smallest, largest):
    def one(axis_at, blocks):
        draws = jax.random.uniform(jax.random.fold_in(jax.random.fold_in(stream_key, 6), axis_at), (blocks,), jnp.float32, smallest / len(cuts), largest / len(cuts))
        return jnp.repeat(jnp.exp(draws), dims[axis_at] // blocks).reshape((-1,) + (1,) * (len(dims) - axis_at - 1))

    factor_of = one(*cuts[0])
    for cut in cuts[1:]:
        factor_of = factor_of * one(*cut)
    return factor_of


def deal_out(stream_key, own, number, rows, count, top, most, skew):
    sequence = jax.random.permutation(stream_key, count)
    crowded, ordinary = portions_of(count, rows * top, most, skew, True), portions_of(count, rows * top, most, skew, False)
    places = jnp.arange(count)

    def named(sizes, offset_by):
        used = int((sizes > 0).sum())
        fixed = max(1, used // 4)
        shifted = fixed + (places - fixed + offset_by * (used - fixed)) % max(1, count - fixed)
        return jnp.zeros((count,), jnp.int32).at[sequence[jnp.where(places < fixed, places, shifted)]].set(jnp.asarray(sizes, jnp.int32))

    sizes = jnp.where(number % 4 == 0, named(crowded, number // 4), named(ordinary, number - number // 4 - 1))
    mixed = jax.random.permutation(jax.random.fold_in(own, 3), count)
    source_of, receiver = mixed[0:count // 2 * 2:2], mixed[1:count // 2 * 2:2]
    slack = jnp.minimum(sizes[source_of] - 1, most - sizes[receiver]) // 2
    slack = jnp.where((source_of == sequence[0]) | (receiver == sequence[0]) | (sizes[receiver] == 0), 0, jnp.maximum(slack, 0))
    shifted = jax.random.randint(jax.random.fold_in(own, 4), (count // 2,), 0, 1 << 20) % (slack + 1)
    sizes = sizes.at[source_of].add(-shifted).at[receiver].add(shifted)
    labels = jnp.searchsorted(jnp.cumsum(sizes), jnp.arange(rows * top), side="right").astype(jnp.int32)
    table = labels.reshape(top, rows).T
    table = table[jax.random.permutation(jax.random.fold_in(own, 1), rows)]
    offset_by = jax.random.randint(jax.random.fold_in(own, 2), (rows, 1), 0, top)
    return jnp.take_along_axis(table, (jnp.arange(top)[None, :] + offset_by) % top, axis=1)


def portions_of(count, total, bound, skew, full):
    weights = [(1 << 20) // math.isqrt(standing ** skew) + 1 for standing in range(1, count + 1)]
    largest = bound if full else min(bound, max(-(-total // count), total * weights[0] // sum(weights)))
    least = 1 if total - largest >= count - 1 else 0
    counts, surplus = [largest] + [least] * (count - 1), total - largest - least * (count - 1)
    while surplus > 0:
        free = [i for i in range(1, count) if counts[i] < largest] or [i for i in range(1, count) if counts[i] < bound]
        mass, remaining = sum([weights[i] for i in free]), surplus
        for i in free:
            more = min(bound - counts[i], max(1, remaining * weights[i] // mass), surplus)
            counts[i] = counts[i] + more
            surplus = surplus - more
    return np.array(counts)


def centred(rng, shape, deviation, limit, cuts=(), held_as=jnp.bfloat16):
    drawn = deviation * jax.random.normal(rng, shape, jnp.float32)
    if cuts:
        drawn = drawn * levels(rng, shape, cuts, -0.22, 0.18)
    return jnp.clip(drawn, -limit, limit).astype(held_as)


def setup_inputs(seed: int = 0) -> dict:
    key_list = jax.random.split(jax.random.key(seed), 16)
    queries = draw_queries(jax.random.fold_in(key_list[15], 71), 0)
    prefix_latents = draw_prefix_latents(jax.random.fold_in(key_list[15], 71), 0)
    new_latents = centred(key_list[2], (PROMPTS, SPAN, KVW), 1.0, 6.0, ((0, 16), (1, 8)))
    prefix_lengths = draw_prefix_lengths(jax.random.fold_in(key_list[15], 71), 0)
    span_sources = draw_span_sources(jax.random.fold_in(key_list[15], 71), 0)
    value_up = centred(key_list[5], (HEADS, LAT, VH), LAT ** -0.5, 0.25, ((0, 8),))
    out_proj = centred(key_list[6], (HEADS * VH, D), VH ** -0.5, 0.5, ((0, 8), (1, 16)))
    residual = draw_residual(jax.random.fold_in(key_list[15], 71), 0)
    norm_gain = jnp.clip(1.0 + 0.18 * jax.random.normal(key_list[8], (D,), jnp.float32), 0.099609375, 1.8984375).astype(jnp.bfloat16)
    expert_gate = centred(key_list[9], (EXPERTS, D, MOE_FF), D ** -0.5, 0.09375, ((0, 128),))
    expert_up = centred(key_list[10], (EXPERTS, D, MOE_FF), D ** -0.5, 0.09375, ((0, 128),))
    expert_down = centred(key_list[11], (EXPERTS, MOE_FF, D), MOE_FF ** -0.5, 0.1875, ((0, 128),))
    expert_ids_keys = jax.random.split(jax.random.fold_in(key_list[12], 1), TOKENS // (SPAN // N_EP))
    expert_ids_turns = jax.random.permutation(jax.random.fold_in(key_list[12], 3), TOKENS // (SPAN // N_EP))
    expert_ids = jax.vmap(lambda own, number: deal_out(jax.random.fold_in(key_list[12], 2), own, number, SPAN // N_EP, EXPERTS, TOP, CAP, 1))(expert_ids_keys, expert_ids_turns).reshape((TOKENS, TOP))
    gate_weights = jnp.clip(0.05 + 0.45 * jax.random.uniform(key_list[13], (TOKENS, TOP), jnp.float32) ** levels(key_list[13], (TOKENS, TOP), ((0, 128),), -0.2, 0.2), 0.05, 0.5)
    decode_owner = jax.random.permutation(key_list[14], PROMPTS).astype(jnp.int32)
    return dict(queries=queries, prefix_latents=prefix_latents, new_latents=new_latents, prefix_lengths=prefix_lengths, span_sources=span_sources, value_up=value_up, out_proj=out_proj, residual=residual, norm_gain=norm_gain, expert_gate=expert_gate, expert_up=expert_up, expert_down=expert_down, expert_ids=expert_ids, gate_weights=gate_weights, decode_owner=decode_owner)


score_scale = 192.0 ** (-0.5)
norm_eps = 1e-06

def attend_rows(query_rows, positions, prefix_rows, new_rows, length):
    query_full = query_rows.astype(jnp.float32)
    key_rows = jnp.concatenate([prefix_rows, new_rows], axis=0).astype(jnp.float32)
    scores = jnp.einsum('thc,jc->thj', query_full, key_rows) * score_scale
    key_pos = lax.broadcasted_iota(jnp.int32, scores.shape, 2)
    tok_pos = positions[:, None, None]
    is_valid = jnp.where(key_pos < PREFIX, key_pos < length, key_pos - PREFIX <= tok_pos)
    scores = jnp.where(is_valid, scores, -1e+30)
    row_max = lax.optimization_barrier(jnp.max(scores, axis=2, keepdims=True))
    expd = jnp.where(is_valid, jnp.exp(scores - row_max), 0.0)
    weight_sum = lax.optimization_barrier(jnp.sum(expd, axis=2, keepdims=True))
    rounded = lax.optimization_barrier(expd.astype(jnp.bfloat16)).astype(jnp.float32)
    weighted = jnp.einsum('thj,jl->thl', rounded, key_rows[:, :LAT])
    return (weighted / weight_sum).astype(jnp.bfloat16)

def reference(queries, prefix_latents, new_latents, prefix_lengths, span_sources, value_up, out_proj, residual, norm_gain, expert_gate, expert_up, expert_down, expert_ids, gate_weights, decode_owner):
    query_blocks = queries.reshape(PROMPTS, SPAN, HEADS, KVW)
    home_rows = SPAN - LATE

    def one_slot(packed):
        block, slot = packed
        source = span_sources[slot]
        first = attend_rows(block[:home_rows], jnp.arange(home_rows, dtype=jnp.int32), prefix_latents[slot], new_latents[slot], prefix_lengths[slot])
        last = attend_rows(block[home_rows:], jnp.arange(home_rows, SPAN, dtype=jnp.int32), prefix_latents[source], new_latents[source], prefix_lengths[source])
        return jnp.concatenate([first, last], axis=0)
    latent_out = lax.map(one_slot, (query_blocks, jnp.arange(PROMPTS, dtype=jnp.int32)))
    latent_out = latent_out.reshape(TOKENS, HEADS, LAT)
    head_rows = jnp.einsum('thl,hlv->thv', latent_out.astype(jnp.float32), value_up.astype(jnp.float32)).astype(jnp.bfloat16)
    head_rows = head_rows.reshape(TOKENS, HEADS * VH)
    attention = jnp.dot(head_rows, out_proj, preferred_element_type=jnp.float32)
    hidden_state = residual.astype(jnp.float32) + attention
    mean_square = lax.optimization_barrier(jnp.mean(hidden_state * hidden_state, axis=1, keepdims=True))
    normed = (hidden_state * lax.rsqrt(mean_square + norm_eps) * norm_gain.astype(jnp.float32)).astype(jnp.bfloat16)
    capacity_rows = N_DP * N_EP * CAP

    def one_expert(running, packed):
        w_gate, w_up, w_down, expert = packed
        routed = expert_ids == expert
        member = jnp.any(routed, axis=1)
        weight = lax.optimization_barrier(jnp.sum(jnp.where(routed, gate_weights.astype(jnp.float32), 0.0), axis=1))
        chosen = jnp.nonzero(member, size=capacity_rows, fill_value=0)[0]
        is_valid = jnp.arange(capacity_rows) < jnp.sum(member.astype(jnp.int32))
        picked_rows = normed[chosen]
        gate_part = jnp.dot(picked_rows, w_gate, preferred_element_type=jnp.float32)
        up_part = jnp.dot(picked_rows, w_up, preferred_element_type=jnp.float32)
        activation = (jax.nn.silu(gate_part) * up_part).astype(jnp.bfloat16)
        expert_out = jnp.dot(activation, w_down, preferred_element_type=jnp.float32).astype(jnp.bfloat16)
        expert_out = lax.optimization_barrier(expert_out).astype(jnp.float32)
        scaled = expert_out * jnp.where(is_valid, weight[chosen], 0.0)[:, None]
        return (running.at[chosen].add(scaled), None)
    moe_total, _ = lax.scan(one_expert, jnp.zeros((TOKENS, D), jnp.float32), (expert_gate, expert_up, expert_down, jnp.arange(EXPERTS, dtype=jnp.int32)))
    layer_out = (hidden_state + moe_total).astype(jnp.bfloat16)
    decode_latents = jnp.zeros_like(new_latents).at[decode_owner].set(new_latents)
    return (layer_out, decode_latents)
```

```python
import jax
import jax.numpy as jnp
from jax import lax
from jax.sharding import PartitionSpec as P

TOP = 8


score_scale = 192.0 ** (-0.5)
norm_eps = 1e-06


def attend(queries, keys, length, positions, prefix_len, latent_width):
    prefix_all = keys[:prefix_len]
    new_all = keys[prefix_len:]
    scores_old = (
        jnp.einsum("thc,jc->thj", queries, prefix_all, preferred_element_type=jnp.float32)
        * score_scale
    )
    scores_new = (
        jnp.einsum("thc,jc->thj", queries, new_all, preferred_element_type=jnp.float32)
        * score_scale
    )
    old_pos = lax.broadcasted_iota(jnp.int32, scores_old.shape, 2)
    old_valid = old_pos < length
    new_pos = lax.broadcasted_iota(jnp.int32, scores_new.shape, 2)
    new_valid = new_pos <= positions[:, None, None]
    scores_old = jnp.where(old_valid, scores_old, -1e30)
    scores_new = jnp.where(new_valid, scores_new, -1e30)
    row_max = jnp.maximum(jnp.max(scores_old, axis=2), jnp.max(scores_new, axis=2))[:, :, None]
    exp_old = jnp.where(old_valid, jnp.exp(scores_old - row_max), 0.0)
    exp_new = jnp.where(new_valid, jnp.exp(scores_new - row_max), 0.0)
    weight_sum = jnp.sum(exp_old, axis=2) + jnp.sum(exp_new, axis=2)
    weighted = jnp.einsum(
        "thj,jl->thl",
        exp_old.astype(jnp.bfloat16),
        prefix_all[:, :latent_width],
        preferred_element_type=jnp.float32,
    )
    weighted = weighted + jnp.einsum(
        "thj,jl->thl",
        exp_new.astype(jnp.bfloat16),
        new_all[:, :latent_width],
        preferred_element_type=jnp.float32,
    )
    return (weighted / weight_sum[:, :, None]).astype(jnp.bfloat16)


def run_local_experts(received, expert_gate, expert_up, expert_down):
    local_experts = expert_gate.shape[0]
    model_width = received.shape[2]
    item_count = received.shape[1]
    grouped = received.reshape(-1, local_experts, item_count, model_width)
    flat_rows = grouped[:, 0].reshape(-1, model_width)
    gate_part = jnp.dot(flat_rows, expert_gate[0], preferred_element_type=jnp.float32)
    up_part = jnp.dot(flat_rows, expert_up[0], preferred_element_type=jnp.float32)
    activation = (jax.nn.silu(gate_part) * up_part).astype(jnp.bfloat16)
    down_part = jnp.dot(activation, expert_down[0], preferred_element_type=jnp.float32)
    results = down_part.astype(jnp.bfloat16).reshape(-1, 1, item_count, model_width)
    return results.reshape(received.shape)


def shards(
    queries,
    prefix_latents,
    new_latents,
    prefix_lengths,
    span_sources,
    value_up,
    out_proj,
    residual,
    norm_gain,
    expert_gate,
    expert_up,
    expert_down,
    expert_ids,
    gate_weights,
    decode_owner,
):
    latent_width = value_up.shape[1]
    model_width = residual.shape[1]
    dp_count = lax.axis_size("dp")
    ep_count = lax.axis_size("ep")
    slot = lax.axis_index("dp")
    span_len = queries.shape[0]
    key_width = queries.shape[2]
    late_rows = span_len // 4
    home_rows = span_len - late_rows
    prefix_part = prefix_latents.shape[1]
    prefix_len = prefix_part * ep_count
    prefix_all, new_all = (
        lax.all_gather(prefix_latents, "ep", axis=1, tiled=True),
        lax.all_gather(new_latents, "ep", axis=1, tiled=True),
    )
    own_keys = jnp.concatenate([prefix_all[0], new_all[0]], axis=0)
    positions = jnp.arange(span_len, dtype=jnp.int32)
    source = span_sources[slot]
    slot_ids = jnp.arange(dp_count, dtype=jnp.int32)
    own_length = prefix_lengths[slot]
    first = attend(
        queries[:home_rows], own_keys, own_length, positions[:home_rows], prefix_len, latent_width
    )
    pieces = jnp.concatenate(
        [
            prefix_latents.reshape(dp_count, -1, key_width),
            new_latents.reshape(dp_count, -1, key_width),
        ],
        axis=1,
    )
    old_rows = prefix_part // dp_count
    spread = lax.all_to_all(pieces, "dp", split_axis=0, concat_axis=0, tiled=True)
    given = jnp.zeros_like(decode_owner).at[decode_owner].set(slot_ids)
    routed = jnp.concatenate([spread[span_sources], spread[given][:, old_rows:]], axis=1)
    arrived = lax.all_to_all(routed, "dp", split_axis=0, concat_axis=0, tiled=True)
    piece_rows = pieces.shape[1]
    moved_shard = jnp.concatenate(
        [
            arrived[:, :old_rows].reshape(-1, key_width),
            arrived[:, old_rows:piece_rows].reshape(-1, key_width),
        ],
        axis=0,
    )
    decode_latents = arrived[:, piece_rows:].reshape(new_latents.shape)
    moved_prefix, moved_new = (
        lax.all_gather(moved_shard[:prefix_part], "ep", axis=0, tiled=True),
        lax.all_gather(moved_shard[prefix_part:], "ep", axis=0, tiled=True),
    )
    moved_keys = jnp.concatenate([moved_prefix, moved_new], axis=0)
    last = attend(
        queries[home_rows:],
        moved_keys,
        prefix_lengths[source],
        positions[home_rows:],
        prefix_len,
        latent_width,
    )
    latent_out = jnp.concatenate([first, last], axis=0)
    head_rows = jnp.einsum(
        "thl,hlv->thv", latent_out, value_up, preferred_element_type=jnp.float32
    ).astype(jnp.bfloat16)
    head_rows = head_rows.reshape(span_len, -1)
    projected = jnp.dot(
        head_rows,
        lax.all_gather(out_proj, "dp", axis=1, tiled=True),
        preferred_element_type=jnp.float32,
    )
    attention = lax.psum_scatter(
        projected.astype(jnp.bfloat16), "ep", scatter_dimension=0, tiled=True
    ).astype(jnp.float32)
    hidden_state = residual.astype(jnp.float32) + attention
    mean_square = jnp.mean(hidden_state * hidden_state, axis=1, keepdims=True)
    normed = (
        hidden_state * lax.rsqrt(mean_square + norm_eps) * norm_gain.astype(jnp.float32)
    ).astype(jnp.bfloat16)
    row_count = expert_ids.shape[0]
    local_experts = expert_gate.shape[0]
    expert_count = local_experts * dp_count * ep_count
    capacity = min(row_count, max(2, row_count * TOP * 4 // (3 * expert_count)))
    route_hits = (
        expert_ids[:, :, None] == jnp.arange(expert_count, dtype=jnp.int32)[None, None, :]
    ).astype(jnp.int32)
    member = jnp.sum(route_hits, axis=1)
    slot_rank = jnp.cumsum(member, axis=0) - member
    target = (slot_rank.T[:, None, :] == jnp.arange(capacity, dtype=jnp.int32)[None, :, None]) & (
        member.T[:, None, :] > 0
    )
    dispatch = jnp.einsum(
        "ecr,rd->ecd", target.astype(jnp.bfloat16), normed, preferred_element_type=jnp.float32
    ).astype(jnp.bfloat16)
    outputs = run_local_experts(
        lax.all_to_all(dispatch, ("dp", "ep"), split_axis=0, concat_axis=0, tiled=True),
        expert_gate,
        expert_up,
        expert_down,
    )
    returned = lax.all_to_all(outputs, ("dp", "ep"), split_axis=0, concat_axis=0, tiled=True)
    route_slot = jnp.take_along_axis(slot_rank, expert_ids, axis=1)
    flat_index = (expert_ids * capacity + route_slot).reshape(-1)
    picked = jnp.take(returned.reshape(-1, model_width), flat_index, axis=0).reshape(
        row_count, -1, model_width
    )
    moe_sum = jnp.sum(gate_weights[:, :, None] * picked.astype(jnp.float32), axis=1)
    layer_out = (hidden_state + moe_sum).astype(jnp.bfloat16)
    return (layer_out, decode_latents)


def solution(mesh):
    return jax.shard_map(
        shards,
        mesh=mesh,
        in_specs=(
            P("dp", "ep", None),
            P("dp", "ep", None),
            P("dp", "ep", None),
            P(),
            P(),
            P("ep", None, None),
            P("ep", "dp"),
            P(("dp", "ep"), None),
            P(),
            P(("dp", "ep"), None, None),
            P(("dp", "ep"), None, None),
            P(("dp", "ep"), None, None),
            P(("dp", "ep"), None),
            P(("dp", "ep"), None),
            P(),
        ),
        out_specs=(P(("dp", "ep"), None), P("dp", "ep", None)),
        check_vma=False,
    )
```

```python
import functools

import jax
import jax.numpy as jnp
from jax import lax
from jax.experimental import pallas as pl
from jax.experimental.pallas import tpu as pltpu
from jax.sharding import PartitionSpec as P

TOP = 8


score_scale = 192.0 ** (-0.5)
norm_eps = 1e-06


def attend(queries, keys, length, positions, prefix_len, latent_width):
    prefix_all = keys[:prefix_len]
    new_all = keys[prefix_len:]
    scores_old = (
        jnp.einsum("thc,jc->thj", queries, prefix_all, preferred_element_type=jnp.float32)
        * score_scale
    )
    scores_new = (
        jnp.einsum("thc,jc->thj", queries, new_all, preferred_element_type=jnp.float32)
        * score_scale
    )
    old_pos = lax.broadcasted_iota(jnp.int32, scores_old.shape, 2)
    old_valid = old_pos < length
    new_pos = lax.broadcasted_iota(jnp.int32, scores_new.shape, 2)
    new_valid = new_pos <= positions[:, None, None]
    scores_old = jnp.where(old_valid, scores_old, -1e30)
    scores_new = jnp.where(new_valid, scores_new, -1e30)
    row_max = jnp.maximum(jnp.max(scores_old, axis=2), jnp.max(scores_new, axis=2))[:, :, None]
    exp_old = jnp.where(old_valid, jnp.exp(scores_old - row_max), 0.0)
    exp_new = jnp.where(new_valid, jnp.exp(scores_new - row_max), 0.0)
    weight_sum = jnp.sum(exp_old, axis=2) + jnp.sum(exp_new, axis=2)
    weighted = jnp.einsum(
        "thj,jl->thl",
        exp_old.astype(jnp.bfloat16),
        prefix_all[:, :latent_width],
        preferred_element_type=jnp.float32,
    )
    weighted = weighted + jnp.einsum(
        "thj,jl->thl",
        exp_new.astype(jnp.bfloat16),
        new_all[:, :latent_width],
        preferred_element_type=jnp.float32,
    )
    return (weighted / weight_sum[:, :, None]).astype(jnp.bfloat16)


MESH = pl.DeviceIdType.MESH


def partners(count, me, each):
    def step(k, carry):
        each(lax.rem(me + k, count))
        return carry

    lax.fori_loop(1, count, step, 0)


def block_rows(start, size):
    return pl.ds(pl.multiple_of(start * size, size), size)


def moe_kernel(
    sizes,
    att_ref,
    res_ref,
    gain_ref,
    ids_ref,
    ids_t_ref,
    gates_ref,
    gate_hbm,
    up_hbm,
    down_hbm,
    out_ref,
    w_gate,
    w_up,
    w_down,
    hid,
    s1,
    r1,
    s2,
    r2,
    total,
    act,
    o1,
    q1,
    q2,
    q3,
    send_sems,
    recv_sems,
    weight_sems,
):
    n_dp, n_ep, chunks = sizes
    dp, ep = lax.axis_index("dp"), lax.axis_index("ep")
    rows = n_dp * n_ep * 2
    dp_block, ep_block = 2 * n_ep, 2 * n_dp
    cols = hid.shape[1] // chunks
    tokens = hid.shape[0]
    hidden_units = w_gate.shape[1]

    loads = [
        pltpu.make_async_copy(src.at[0], dst, weight_sems.at[i])
        for i, (src, dst) in enumerate(((gate_hbm, w_gate), (up_hbm, w_up), (down_hbm, w_down)))
    ]
    for load in loads:
        load.start()

    barrier = pltpu.get_barrier_semaphore()
    partners(
        n_dp,
        dp,
        lambda p: pl.semaphore_signal(barrier, inc=1, device_id=(p, ep), device_id_type=MESH),
    )
    partners(
        n_ep,
        ep,
        lambda p: pl.semaphore_signal(barrier, inc=1, device_id=(dp, p), device_id_type=MESH),
    )

    def send_dp(stage, c, src, dst):
        def each(p):
            pltpu.make_async_remote_copy(
                src_ref=src.at[c, block_rows(p, dp_block)],
                dst_ref=dst.at[c, block_rows(dp, dp_block)],
                send_sem=send_sems.at[stage, c],
                recv_sem=recv_sems.at[stage, c],
                device_id=(p, ep),
                device_id_type=MESH,
            ).start()

        partners(n_dp, dp, each)
        dst[c, block_rows(dp, dp_block)] = src[c, block_rows(dp, dp_block)]

    def send_ep(stage, c, src, dst):
        def each(p):
            pltpu.make_async_remote_copy(
                src_ref=src.at[c, block_rows(p, ep_block)],
                dst_ref=dst.at[c, block_rows(ep, ep_block)],
                send_sem=send_sems.at[stage, c],
                recv_sem=recv_sems.at[stage, c],
                device_id=(dp, p),
                device_id_type=MESH,
            ).start()

        partners(n_ep, ep, each)
        dst[c, block_rows(ep, ep_block)] = src[c, block_rows(ep, ep_block)]

    def wait_all(sems, stage, c, ref):
        size = rows - (dp_block if stage in (0, 3) else ep_block)
        part = ref.at[c, pl.ds(0, size)]
        pltpu.make_async_copy(part, part, sems.at[stage, c]).wait()

    def mm(a, b):
        return jnp.dot(a, b, preferred_element_type=jnp.float32)

    slot_col = lax.broadcasted_iota(jnp.int32, (rows, tokens), 0)
    slot_row = lax.broadcasted_iota(jnp.int32, (tokens, rows), 1)
    named_t = jnp.zeros((rows, tokens), jnp.float32)
    named = jnp.zeros((tokens, rows), jnp.float32)
    weight = jnp.zeros((tokens, rows), jnp.float32)
    for k in range(TOP):
        named_t += jnp.where(ids_t_ref[k : k + 1, :] == (slot_col >> 1), 1.0, 0.0)
        hit = ids_ref[:, k : k + 1] == (slot_row >> 1)
        named += jnp.where(hit, 1.0, 0.0)
        weight += jnp.where(hit, gates_ref[:, k : k + 1], 0.0)
    first = lax.broadcasted_iota(jnp.int32, (tokens, tokens), 0)
    second = lax.broadcasted_iota(jnp.int32, (tokens, tokens), 1)
    before_t = jnp.where(first < second, 1.0, 0.0).astype(jnp.bfloat16)
    before = jnp.where(second < first, 1.0, 0.0).astype(jnp.bfloat16)
    rank_t = mm(named_t.astype(jnp.bfloat16), before_t)
    rank = mm(before, named.astype(jnp.bfloat16))
    pick = jnp.where(rank_t == (slot_col & 1).astype(jnp.float32), named_t, 0.0).astype(
        jnp.bfloat16
    )
    weight = jnp.where(rank == (slot_row & 1).astype(jnp.float32), weight, 0.0)
    weight_high = weight.astype(jnp.bfloat16)
    weight_low = (weight - weight_high.astype(jnp.float32)).astype(jnp.bfloat16)
    weights = jnp.concatenate([weight_high, weight_low], axis=0)
    to = lax.broadcasted_iota(jnp.int32, (rows, rows), 0)
    frm = lax.broadcasted_iota(jnp.int32, (rows, rows), 1)
    by_ep = lax.rem(to >> 1, n_dp) * dp_block + (to // ep_block) * 2 + (to & 1)
    by_dp = lax.rem(to >> 1, n_ep) * ep_block + (to // dp_block) * 2 + (to & 1)
    perm_ep = jnp.where(frm == by_ep, 1.0, 0.0).astype(jnp.bfloat16)
    perm_dp = jnp.where(frm == by_dp, 1.0, 0.0).astype(jnp.bfloat16)

    hidden = res_ref[...].astype(jnp.float32) + att_ref[...].astype(jnp.float32)
    hid[...] = hidden
    mean_square = jnp.mean(hidden * hidden, axis=1, keepdims=True)
    scale = lax.rsqrt(mean_square + norm_eps)

    pl.semaphore_wait(barrier, n_dp + n_ep - 2)

    for c in range(chunks):
        span = pl.ds(c * cols, cols)
        normed = (hid[:, span] * scale * gain_ref[:, span].astype(jnp.float32)).astype(
            jnp.bfloat16
        )
        s1[c] = mm(pick, normed).astype(jnp.bfloat16)
        send_dp(0, c, s1, r1)
    for c in range(chunks):
        wait_all(recv_sems, 0, c, r1)
        s2[c] = mm(perm_ep, r1[c]).astype(jnp.bfloat16)
        send_ep(1, c, s2, r2)
    loads[0].wait()
    loads[1].wait()
    for c in range(chunks):
        wait_all(recv_sems, 1, c, r2)
        span = pl.ds(c * cols, cols)
        x = r2[c]
        gate_part = mm(x, w_gate[span, :])
        up_part = mm(x, w_up[span, :])
        if c:
            gate_part += total[:, pl.ds(0, hidden_units)]
            up_part += total[:, pl.ds(hidden_units, hidden_units)]
        if c < chunks - 1:
            total[:, pl.ds(0, hidden_units)] = gate_part
            total[:, pl.ds(hidden_units, hidden_units)] = up_part
        else:
            act[...] = (gate_part / (1.0 + jnp.exp(-gate_part)) * up_part).astype(jnp.bfloat16)
    loads[2].wait()
    for c in range(chunks):
        o1[c] = mm(act[...], w_down[:, pl.ds(c * cols, cols)]).astype(jnp.bfloat16)
        send_ep(2, c, o1, q1)
    for c in range(chunks):
        wait_all(recv_sems, 2, c, q1)
        q2[c] = mm(perm_dp, q1[c]).astype(jnp.bfloat16)
        send_dp(3, c, q2, q3)
    for c in range(chunks):
        wait_all(recv_sems, 3, c, q3)
        span = pl.ds(c * cols, cols)
        both = mm(weights, q3[c])
        out_ref[:, span] = (hid[:, span] + (both[:tokens] + both[tokens:])).astype(out_ref.dtype)
    for stage, ref in enumerate((s1, s2, o1, q2)):
        for c in range(chunks):
            wait_all(send_sems, stage, c, ref)


def moe(attention, residual, norm_gain, expert_ids, gate_weights, expert_gate, expert_up, expert_down):
    n_dp, n_ep = lax.axis_size("dp"), lax.axis_size("ep")
    tokens, width = residual.shape
    units = expert_gate.shape[2]
    rows = n_dp * n_ep * 2
    chunks = 4
    buf = pltpu.VMEM((chunks, rows, width // chunks), jnp.bfloat16)
    vmem = pl.BlockSpec(memory_space=pltpu.VMEM)
    hbm = pl.BlockSpec(memory_space=pl.ANY)
    return pl.pallas_call(
        functools.partial(moe_kernel, (n_dp, n_ep, chunks)),
        out_shape=jax.ShapeDtypeStruct((tokens, width), jnp.bfloat16),
        in_specs=[vmem] * 6 + [hbm] * 3,
        out_specs=vmem,
        scratch_shapes=[
            pltpu.VMEM((width, units), jnp.bfloat16),
            pltpu.VMEM((width, units), jnp.bfloat16),
            pltpu.VMEM((units, width), jnp.bfloat16),
            pltpu.VMEM((tokens, width), jnp.float32),
            buf,
            buf,
            buf,
            buf,
            pltpu.VMEM((rows, 2 * units), jnp.float32),
            pltpu.VMEM((rows, units), jnp.bfloat16),
            buf,
            buf,
            buf,
            buf,
            pltpu.SemaphoreType.DMA((4, chunks)),
            pltpu.SemaphoreType.DMA((4, chunks)),
            pltpu.SemaphoreType.DMA((3,)),
        ],
        compiler_params=pltpu.CompilerParams(
            collective_id=1, has_side_effects=True, vmem_limit_bytes=60 * 2**20
        ),
        name="experts",
    )(
        attention,
        residual,
        norm_gain.reshape(1, -1),
        expert_ids,
        expert_ids.T,
        gate_weights,
        expert_gate,
        expert_up,
        expert_down,
    )


def shards(
    queries,
    prefix_latents,
    new_latents,
    prefix_lengths,
    span_sources,
    value_up,
    out_proj,
    residual,
    norm_gain,
    expert_gate,
    expert_up,
    expert_down,
    expert_ids,
    gate_weights,
    decode_owner,
):
    latent_width = value_up.shape[1]
    model_width = residual.shape[1]
    dp_count = lax.axis_size("dp")
    ep_count = lax.axis_size("ep")
    slot = lax.axis_index("dp")
    span_len = queries.shape[0]
    key_width = queries.shape[2]
    late_rows = span_len // 4
    home_rows = span_len - late_rows
    prefix_part = prefix_latents.shape[1]
    prefix_len = prefix_part * ep_count
    prefix_all, new_all = (
        lax.all_gather(prefix_latents, "ep", axis=1, tiled=True),
        lax.all_gather(new_latents, "ep", axis=1, tiled=True),
    )
    own_keys = jnp.concatenate([prefix_all[0], new_all[0]], axis=0)
    positions = jnp.arange(span_len, dtype=jnp.int32)
    source = span_sources[slot]
    slot_ids = jnp.arange(dp_count, dtype=jnp.int32)
    own_length = prefix_lengths[slot]
    first = attend(
        queries[:home_rows], own_keys, own_length, positions[:home_rows], prefix_len, latent_width
    )
    pieces = jnp.concatenate(
        [
            prefix_latents.reshape(dp_count, -1, key_width),
            new_latents.reshape(dp_count, -1, key_width),
        ],
        axis=1,
    )
    old_rows = prefix_part // dp_count
    spread = lax.all_to_all(pieces, "dp", split_axis=0, concat_axis=0, tiled=True)
    given = jnp.zeros_like(decode_owner).at[decode_owner].set(slot_ids)
    routed = jnp.concatenate([spread[span_sources], spread[given][:, old_rows:]], axis=1)
    arrived = lax.all_to_all(routed, "dp", split_axis=0, concat_axis=0, tiled=True)
    piece_rows = pieces.shape[1]
    moved_shard = jnp.concatenate(
        [
            arrived[:, :old_rows].reshape(-1, key_width),
            arrived[:, old_rows:piece_rows].reshape(-1, key_width),
        ],
        axis=0,
    )
    decode_latents = arrived[:, piece_rows:].reshape(new_latents.shape)
    moved_prefix, moved_new = (
        lax.all_gather(moved_shard[:prefix_part], "ep", axis=0, tiled=True),
        lax.all_gather(moved_shard[prefix_part:], "ep", axis=0, tiled=True),
    )
    moved_keys = jnp.concatenate([moved_prefix, moved_new], axis=0)
    last = attend(
        queries[home_rows:],
        moved_keys,
        prefix_lengths[source],
        positions[home_rows:],
        prefix_len,
        latent_width,
    )
    latent_out = jnp.concatenate([first, last], axis=0)
    head_rows = jnp.einsum(
        "thl,hlv->thv", latent_out, value_up, preferred_element_type=jnp.float32
    ).astype(jnp.bfloat16)
    head_rows = head_rows.reshape(span_len, -1)
    projected = jnp.dot(
        head_rows,
        lax.all_gather(out_proj, "dp", axis=1, tiled=True),
        preferred_element_type=jnp.float32,
    )
    attention = lax.psum_scatter(
        projected.astype(jnp.bfloat16), "ep", scatter_dimension=0, tiled=True
    )
    layer_out = moe(
        attention,
        residual,
        norm_gain,
        expert_ids,
        gate_weights,
        expert_gate,
        expert_up,
        expert_down,
    )
    return (layer_out, decode_latents)


def solution(mesh):
    return jax.shard_map(
        shards,
        mesh=mesh,
        in_specs=(
            P("dp", "ep", None),
            P("dp", "ep", None),
            P("dp", "ep", None),
            P(),
            P(),
            P("ep", None, None),
            P("ep", "dp"),
            P(("dp", "ep"), None),
            P(),
            P(("dp", "ep"), None, None),
            P(("dp", "ep"), None, None),
            P(("dp", "ep"), None, None),
            P(("dp", "ep"), None),
            P(("dp", "ep"), None),
            P(),
        ),
        out_specs=(P(("dp", "ep"), None), P("dp", "ep", None)),
        check_vma=False,
    )
```

```python
import functools
import math

import jax
import jax.numpy as jnp
from jax import lax
from jax.experimental import pallas as pl
from jax.experimental.pallas import tpu as pltpu
from jax.sharding import PartitionSpec as P

TOP = 8


score_scale = 192.0 ** (-0.5)
exp2_scale = score_scale * math.log2(math.e)
norm_eps = 1e-06


MESH = pl.DeviceIdType.MESH


def partners(count, me, each):
    def step(k, carry):
        each(lax.rem(me + k, count))
        return carry

    lax.fori_loop(1, count, step, 0)


def block_rows(start, size):
    return pl.ds(pl.multiple_of(start * size, size), size)


def moe_kernel(
    sizes,
    att_ref,
    res_ref,
    gain_ref,
    ids_ref,
    gates_ref,
    gate_hbm,
    up_hbm,
    down_hbm,
    out_ref,
    w_gate,
    w_up,
    w_down,
    hid,
    s1,
    r1,
    s2,
    r2,
    total,
    act,
    o1,
    q1,
    q2,
    q3,
    send_sems,
    recv_sems,
    weight_sems,
):
    n_dp, n_ep, chunks = sizes
    dp, ep = lax.axis_index("dp"), lax.axis_index("ep")
    rows = n_dp * n_ep * 2
    dp_block, ep_block = 2 * n_ep, 2 * n_dp
    cols = hid.shape[1] // chunks
    tokens = hid.shape[0]
    hidden_units = w_gate.shape[1]

    loads = [
        pltpu.make_async_copy(src.at[0], dst, weight_sems.at[i])
        for i, (src, dst) in enumerate(((gate_hbm, w_gate), (up_hbm, w_up), (down_hbm, w_down)))
    ]
    for load in loads:
        load.start()

    barrier = pltpu.get_barrier_semaphore()
    partners(
        n_dp,
        dp,
        lambda p: pl.semaphore_signal(barrier, inc=1, device_id=(p, ep), device_id_type=MESH),
    )
    partners(
        n_ep,
        ep,
        lambda p: pl.semaphore_signal(barrier, inc=1, device_id=(dp, p), device_id_type=MESH),
    )

    def send_dp(stage, c, src, dst):
        def each(p):
            pltpu.make_async_remote_copy(
                src_ref=src.at[c, block_rows(p, dp_block)],
                dst_ref=dst.at[c, block_rows(dp, dp_block)],
                send_sem=send_sems.at[stage, c],
                recv_sem=recv_sems.at[stage, c],
                device_id=(p, ep),
                device_id_type=MESH,
            ).start()

        partners(n_dp, dp, each)
        dst[c, block_rows(dp, dp_block)] = src[c, block_rows(dp, dp_block)]

    def send_ep(stage, c, src, dst):
        def each(p):
            pltpu.make_async_remote_copy(
                src_ref=src.at[c, block_rows(p, ep_block)],
                dst_ref=dst.at[c, block_rows(ep, ep_block)],
                send_sem=send_sems.at[stage, c],
                recv_sem=recv_sems.at[stage, c],
                device_id=(dp, p),
                device_id_type=MESH,
            ).start()

        partners(n_ep, ep, each)
        dst[c, block_rows(ep, ep_block)] = src[c, block_rows(ep, ep_block)]

    def wait_all(sems, stage, c, ref):
        size = rows - (dp_block if stage in (0, 3) else ep_block)
        part = ref.at[c, pl.ds(0, size)]
        pltpu.make_async_copy(part, part, sems.at[stage, c]).wait()

    def mm(a, b):
        return jnp.dot(a, b, preferred_element_type=jnp.float32)

    slot = lax.broadcasted_iota(jnp.int32, (rows, tokens), 0)
    named = jnp.zeros((rows, tokens), jnp.float32)
    weight = jnp.zeros((rows, tokens), jnp.float32)
    for k in range(TOP):
        hit = ids_ref[k : k + 1, :] == (slot >> 1)
        named += jnp.where(hit, 1.0, 0.0)
        weight += jnp.where(hit, gates_ref[k : k + 1, :], 0.0)
    first = lax.broadcasted_iota(jnp.int32, (tokens, tokens), 0)
    second = lax.broadcasted_iota(jnp.int32, (tokens, tokens), 1)
    before = jnp.where(first < second, 1.0, 0.0).astype(jnp.bfloat16)
    same = jnp.where(first == second, 1.0, 0.0).astype(jnp.bfloat16)
    chosen = mm(named.astype(jnp.bfloat16), before) == (slot & 1).astype(jnp.float32)
    pick = jnp.where(chosen, named, 0.0).astype(jnp.bfloat16)
    weight = jnp.where(chosen, weight, 0.0)
    weight_high = weight.astype(jnp.bfloat16)
    weight_low = (weight - weight_high.astype(jnp.float32)).astype(jnp.bfloat16)
    weight_high = contract_last(same, weight_high).astype(jnp.bfloat16)
    weight_low = contract_last(same, weight_low).astype(jnp.bfloat16)
    weights = jnp.concatenate([weight_high, weight_low], axis=0)
    to = lax.broadcasted_iota(jnp.int32, (rows, rows), 0)
    frm = lax.broadcasted_iota(jnp.int32, (rows, rows), 1)
    by_ep = lax.rem(to >> 1, n_dp) * dp_block + (to // ep_block) * 2 + (to & 1)
    by_dp = lax.rem(to >> 1, n_ep) * ep_block + (to // dp_block) * 2 + (to & 1)
    perm_ep = jnp.where(frm == by_ep, 1.0, 0.0).astype(jnp.bfloat16)
    perm_dp = jnp.where(frm == by_dp, 1.0, 0.0).astype(jnp.bfloat16)

    hidden = res_ref[...].astype(jnp.float32) + att_ref[...].astype(jnp.float32)
    hid[...] = hidden
    mean_square = jnp.mean(hidden * hidden, axis=1, keepdims=True)
    scale = lax.rsqrt(mean_square + norm_eps)

    pl.semaphore_wait(barrier, n_dp + n_ep - 2)

    for c in range(chunks):
        span = pl.ds(c * cols, cols)
        normed = (hid[:, span] * scale * gain_ref[:, span].astype(jnp.float32)).astype(
            jnp.bfloat16
        )
        s1[c] = mm(pick, normed).astype(jnp.bfloat16)
        send_dp(0, c, s1, r1)
    for c in range(chunks):
        wait_all(recv_sems, 0, c, r1)
        s2[c] = mm(perm_ep, r1[c]).astype(jnp.bfloat16)
        send_ep(1, c, s2, r2)
    loads[0].wait()
    loads[1].wait()
    for c in range(chunks):
        wait_all(recv_sems, 1, c, r2)
        span = pl.ds(c * cols, cols)
        x = r2[c]
        gate_part = mm(x, w_gate[span, :])
        up_part = mm(x, w_up[span, :])
        if c:
            gate_part += total[:, pl.ds(0, hidden_units)]
            up_part += total[:, pl.ds(hidden_units, hidden_units)]
        if c < chunks - 1:
            total[:, pl.ds(0, hidden_units)] = gate_part
            total[:, pl.ds(hidden_units, hidden_units)] = up_part
        else:
            act[...] = (gate_part / (1.0 + jnp.exp(-gate_part)) * up_part).astype(jnp.bfloat16)
    loads[2].wait()
    for c in range(chunks):
        o1[c] = mm(act[...], w_down[:, pl.ds(c * cols, cols)]).astype(jnp.bfloat16)
        send_ep(2, c, o1, q1)
    for c in range(chunks):
        wait_all(recv_sems, 2, c, q1)
        q2[c] = mm(perm_dp, q1[c]).astype(jnp.bfloat16)
        send_dp(3, c, q2, q3)
    for c in range(chunks):
        wait_all(recv_sems, 3, c, q3)
        span = pl.ds(c * cols, cols)
        both = mm(weights, q3[c])
        out_ref[:, span] = (hid[:, span] + (both[:tokens] + both[tokens:])).astype(out_ref.dtype)
    for stage, ref in enumerate((s1, s2, o1, q2)):
        for c in range(chunks):
            wait_all(send_sems, stage, c, ref)


def moe(attention, residual, norm_gain, expert_ids, gate_weights, expert_gate, expert_up, expert_down):
    n_dp, n_ep = lax.axis_size("dp"), lax.axis_size("ep")
    tokens, width = residual.shape
    units = expert_gate.shape[2]
    rows = n_dp * n_ep * 2
    chunks = 4
    buf = pltpu.VMEM((chunks, rows, width // chunks), jnp.bfloat16)
    vmem = pl.BlockSpec(memory_space=pltpu.VMEM)
    hbm = pl.BlockSpec(memory_space=pl.ANY)
    return pl.pallas_call(
        functools.partial(moe_kernel, (n_dp, n_ep, chunks)),
        out_shape=jax.ShapeDtypeStruct((tokens, width), jnp.bfloat16),
        in_specs=[vmem] * 5 + [hbm] * 3,
        out_specs=vmem,
        scratch_shapes=[
            pltpu.VMEM((width, units), jnp.bfloat16),
            pltpu.VMEM((width, units), jnp.bfloat16),
            pltpu.VMEM((units, width), jnp.bfloat16),
            pltpu.VMEM((tokens, width), jnp.float32),
            buf,
            buf,
            buf,
            buf,
            pltpu.VMEM((rows, 2 * units), jnp.float32),
            pltpu.VMEM((rows, units), jnp.bfloat16),
            buf,
            buf,
            buf,
            buf,
            pltpu.SemaphoreType.DMA((4, chunks)),
            pltpu.SemaphoreType.DMA((4, chunks)),
            pltpu.SemaphoreType.DMA((3,)),
        ],
        compiler_params=pltpu.CompilerParams(
            collective_id=1, has_side_effects=True, vmem_limit_bytes=60 * 2**20
        ),
        name="experts",
    )(
        attention,
        residual,
        norm_gain.reshape(1, -1),
        expert_ids.T,
        gate_weights.T,
        expert_gate,
        expert_up,
        expert_down,
    )


def contract_last(a, b):
    return lax.dot_general(a, b, (((1,), (1,)), ((), ())), preferred_element_type=jnp.float32)


def attend(q, keys, length, positions, prefix_len, lat):
    s_old = contract_last(q, keys[0:prefix_len, :])
    s_new = contract_last(q, keys[prefix_len:, :])
    old_pos = lax.broadcasted_iota(jnp.int32, (1, prefix_len), 1)
    s_old = s_old + jnp.where(old_pos < length, 0.0, -1e30)
    new_pos = lax.broadcasted_iota(jnp.int32, s_new.shape, 1)
    s_new = jnp.where(new_pos <= positions, s_new, -1e30)
    top = jnp.maximum(
        jnp.max(s_old, axis=1, keepdims=True), jnp.max(s_new, axis=1, keepdims=True)
    )
    e_old = jnp.exp2((s_old - top) * exp2_scale)
    e_new = jnp.exp2((s_new - top) * exp2_scale)
    weight_sum = jnp.sum(e_old, axis=1, keepdims=True) + jnp.sum(e_new, axis=1, keepdims=True)
    weighted = jnp.dot(
        e_old.astype(jnp.bfloat16), keys[0:prefix_len, 0:lat], preferred_element_type=jnp.float32
    )
    weighted += jnp.dot(
        e_new.astype(jnp.bfloat16), keys[prefix_len:, 0:lat], preferred_element_type=jnp.float32
    )
    return (weighted * (1.0 / weight_sum)).astype(jnp.bfloat16)


SIDE = 4


def attention_kernel(
    lengths_ref,
    sources_ref,
    owner_ref,
    prefix_ref,
    new_ref,
    proj_ref,
    queries_hbm,
    value_up_hbm,
    att_ref,
    decode_ref,
    q_raw,
    value_up,
    q_home,
    q_late,
    keys_own,
    keys_moved,
    spread,
    staged,
    news,
    proj,
    heads,
    part,
    part_b,
    pair,
    summed,
    gathered,
    z_recv,
    y_recv,
    dp_recv,
    x_recv,
    pair_recv,
    last_recv,
    sends,
    load_sems,
):
    dp, ep = lax.axis_index("dp"), lax.axis_index("ep")
    x, y = dp // SIDE, lax.rem(dp, SIDE)
    z, core = ep // 2, lax.rem(ep, 2)
    n_dp = SIDE * SIDE
    n_ep = 2 * SIDE
    prefix_part, new_part = prefix_ref.shape[2], new_ref.shape[1]
    prefix_len = prefix_part * n_ep
    shard_rows = prefix_part + new_part
    head_count, lat, vh = value_up.shape
    span = q_raw.shape[2]
    late = span // 4
    home = span - late
    tokens = span // n_ep
    col_part = proj_ref.shape[0]
    cols = col_part * SIDE
    piece = prefix_part // n_dp

    def around(a, k):
        return lax.rem(a + k + SIDE, SIDE)

    def device(x2, y2, z2, core2):
        return (x2 * SIDE + y2, z2 * 2 + core2)

    right_z, left_z = device(x, y, around(z, 1), core), device(x, y, around(z, -1), core)
    right_y, left_y = device(x, around(y, 1), z, core), device(x, around(y, -1), z, core)
    sibling = device(x, y, z, 1 - core)

    load_q = pltpu.make_async_copy(queries_hbm, q_raw, load_sems.at[0])
    load_q.start()
    load_v = pltpu.make_async_copy(value_up_hbm, value_up, load_sems.at[1])
    load_v.start()

    barrier = pltpu.get_barrier_semaphore()

    def hello(to):
        pl.semaphore_signal(barrier, inc=1, device_id=to, device_id_type=MESH)

    partners(n_dp, dp, lambda p: hello((p, ep)))
    for kz in range(1, SIDE):
        for kx in range(SIDE):
            hello(device(around(x, kx), y, around(z, kz), core))
    hello(sibling)

    def send(src, dst, to, send_sem, recv_sem):
        pltpu.make_async_remote_copy(
            src_ref=src,
            dst_ref=dst,
            send_sem=send_sem,
            recv_sem=recv_sem,
            device_id=to,
            device_id_type=MESH,
        ).start()

    def wait(sem, ref):
        pltpu.make_async_copy(ref, ref, sem).wait()

    def key_parts(buf, z2, core2, half):
        at = z2 * 2 + core2
        n, m = (prefix_part // 2, new_part // 2) if half is not None else (prefix_part, new_part)
        half = half or 0
        old = pl.multiple_of(at * prefix_part + half * n, n)
        new = pl.multiple_of(prefix_len + at * new_part + half * m, m)
        return [buf.at[pl.ds(old, n)], buf.at[pl.ds(new, m)]]

    eye_a = lax.broadcasted_iota(jnp.int32, (span, span), 0)
    eye_b = lax.broadcasted_iota(jnp.int32, (span, span), 1)
    eye = jnp.where(eye_a == eye_b, 1.0, 0.0).astype(jnp.bfloat16)
    keys_own[block_rows(ep, prefix_part)] = contract_last(eye, prefix_ref[0]).astype(jnp.bfloat16)
    keys_own[pl.ds(pl.multiple_of(prefix_len + ep * new_part, new_part), new_part)] = new_ref[0]
    proj[block_rows(y, col_part)] = proj_ref[...]

    pl.semaphore_wait(barrier, n_dp - 1 + (SIDE - 1) * SIDE + 1)

    def ring_start(refs, right, left, send_sem, recv):
        for half in (0, 1):
            for ref in refs(0, half):
                send(ref, ref, right, send_sem, recv.at[half])
            for ref in refs(0, 1 - half):
                send(ref, ref, left, send_sem, recv.at[2 + 1 - half])

    def ring_forward(refs, right, left, send_sem, recv, half_ref):
        wait(recv.at[0], half_ref)
        for ref in refs(-1, 0):
            send(ref, ref, right, send_sem, recv.at[4])
        wait(recv.at[3], half_ref)
        for ref in refs(1, 1):
            send(ref, ref, left, send_sem, recv.at[5])

    class Keys:
        def __init__(self, i, buf):
            self.i, self.buf = i, buf
            self.recv = z_recv.at[i]
            self.half = buf.at[pl.ds(0, shard_rows // 2)]
            self.full = buf.at[pl.ds(0, shard_rows)]

        def refs(self, k, half):
            return key_parts(self.buf, around(z, k), core, half)

        def start(self):
            ring_start(self.refs, right_z, left_z, sends.at[self.i], self.recv)
            self.share(0, 6)

        def share(self, k, sem):
            for ref in self.refs(k, None):
                send(ref, ref, sibling, sends.at[self.i], self.recv.at[sem])

        def forward(self):
            ring_forward(self.refs, right_z, left_z, sends.at[self.i], self.recv, self.half)

        def forward_near(self):
            wait(self.recv.at[1], self.half)
            self.share(-1, 7)
            wait(self.recv.at[2], self.half)
            self.share(1, 8)

        def forward_far(self):
            wait(self.recv.at[4], self.half)
            wait(self.recv.at[5], self.half)
            self.share(2, 9)

        def finish(self):
            for sem in range(6, 10):
                wait(self.recv.at[sem], self.full)

    own, moved = Keys(0, keys_own), Keys(1, keys_moved)

    own.start()
    prefix_at = ep * prefix_part

    def spread_to(p):
        rows = pl.multiple_of(prefix_at + p * piece, piece)
        send(keys_own.at[pl.ds(rows, piece)], spread.at[dp], (p, ep), sends.at[2], dp_recv.at[0])

    partners(n_dp, dp, spread_to)
    spread[dp] = keys_own[pl.ds(pl.multiple_of(prefix_at + dp * piece, piece), piece)]
    news[dp] = new_ref[0]
    partners(
        n_dp,
        dp,
        lambda p: send(news.at[dp], news.at[dp], (p, ep), sends.at[3], dp_recv.at[1]),
    )

    def proj_refs(k, half):
        n = col_part // 2
        start = pl.multiple_of(around(y, k) * col_part + half * n, n)
        return [proj.at[pl.ds(start, n)]]

    ring_start(proj_refs, right_y, left_y, sends.at[4], y_recv)

    load_q.wait()

    def turn_head(h):
        rows = contract_last(eye, q_raw[h]).astype(jnp.bfloat16)
        q_home[h // 2, pl.ds((h % 2) * home, home)] = rows[:home]
        q_late[pl.ds(h * late, late)] = rows[home:]

    for h in range(head_count // 2):
        turn_head(h)
    own.forward()
    wait(dp_recv.at[0], keys_own.at[pl.ds(0, prefix_part - piece)])

    def stage(s, carry):
        staged[s] = spread[sources_ref[s]]
        return carry

    lax.fori_loop(0, n_dp, stage, 0)
    landing = keys_moved.at[pl.ds(pl.multiple_of(prefix_at + dp * piece, piece), piece)]
    partners(
        n_dp,
        dp,
        lambda p: send(staged.at[p], landing, (p, ep), sends.at[5], dp_recv.at[2]),
    )
    keys_moved[pl.ds(pl.multiple_of(prefix_at + dp * piece, piece), piece)] = staged[dp]
    for h in range(head_count // 2, head_count):
        turn_head(h)
    own.forward_near()
    source = sources_ref[dp]
    given = jnp.int32(0)
    for i in range(n_dp):
        given = jnp.maximum(given, jnp.where(owner_ref[i] == dp, i, 0))
    wait(dp_recv.at[1], keys_own.at[pl.ds(0, (n_dp - 1) * new_part)])
    decode_ref[0] = news[given]
    keys_moved[pl.ds(pl.multiple_of(prefix_len + ep * new_part, new_part), new_part)] = news[source]
    wait(dp_recv.at[2], keys_own.at[pl.ds(0, prefix_part - piece)])
    moved.start()
    own.forward_far()
    ring_forward(proj_refs, right_y, left_y, sends.at[4], y_recv, proj.at[pl.ds(0, col_part // 2)])
    own.finish()
    load_v.wait()

    def send_heads(i, rows, lanes):
        for k in (2, 1, 3):
            ref = heads.at[x, rows, lanes]
            send(ref, ref, device(around(x, k), y, z, core), sends.at[6 + i], x_recv.at[i])

    home_row = lax.broadcasted_iota(jnp.int32, (2 * home, 1), 0)
    home_pos = jnp.where(home_row >= home, home_row - home, home_row)
    pairs = head_count // 2
    for i in range(pairs):
        out = attend(q_home[i], keys_own, lengths_ref[dp], home_pos, prefix_len, lat)
        for j in range(2):
            h = 2 * i + j
            heads[x, pl.ds(0, home), pl.ds(h * vh, vh)] = jnp.dot(
                out[j * home : (j + 1) * home], value_up[h], preferred_element_type=jnp.float32
            ).astype(jnp.bfloat16)
        send_heads(i, pl.ds(0, home), pl.ds(2 * i * vh, 2 * vh))
        if i == 0:
            moved.forward()
        if i == 1:
            moved.forward_near()
        if i == 2:
            moved.forward_far()
    moved.finish()
    late_row = lax.broadcasted_iota(jnp.int32, (head_count * late, 1), 0)
    late_pos = lax.rem(late_row, late) + home
    out = attend(q_late[...], keys_moved, lengths_ref[source], late_pos, prefix_len, lat)
    for h in range(head_count):
        heads[x, pl.ds(home, late), pl.ds(h * vh, vh)] = jnp.dot(
            out[h * late : (h + 1) * late], value_up[h], preferred_element_type=jnp.float32
        ).astype(jnp.bfloat16)
    send_heads(pairs, pl.ds(home, late), pl.ds(0, head_count * vh))

    for i in (1, 2, 4, 5):
        wait(y_recv.at[i], proj.at[pl.ds(0, col_part // 2)])

    order = (0, 2, 1, 3)

    def project(k):
        xk = around(x, k)
        out = contract_last(heads[xk], proj[...])
        part[xk] = out
        part_b[xk] = out.astype(jnp.bfloat16)
        for kz in range(SIDE):
            rows = block_rows(kz * 2 + 1 - core, tokens)
            send(
                part_b.at[xk, rows],
                pair.at[xk, pl.ds(kz * tokens, tokens)],
                sibling,
                sends.at[11],
                pair_recv.at[k],
            )

    def pass_on(k):
        xk = around(x, k)
        wait(pair_recv.at[k], pair.at[0])
        for kz in (2, 1, 3, 0):
            zk = around(z, kz)
            mine = part[xk, block_rows(zk * 2 + core, tokens)]
            both = mine + pair[xk, block_rows(zk, tokens)].astype(jnp.float32)
            both = both.astype(jnp.bfloat16)
            if k == 0 and kz == 0:
                gathered[block_rows(x * SIDE + z, tokens)] = both
                continue
            at = block_rows(xk * SIDE + zk, tokens)
            summed[at] = both
            send(
                summed.at[at],
                gathered.at[block_rows(x * SIDE + z, tokens)],
                device(xk, y, zk, core),
                sends.at[12],
                last_recv,
            )

    project(0)
    wait(x_recv.at[pairs], heads.at[0, pl.ds(0, 3 * late)])
    for i in range(pairs):
        wait(x_recv.at[i], heads.at[0, pl.ds(0, 3 * home * 2 // head_count)])
    project(2)
    project(1)
    pass_on(2)
    project(3)
    pass_on(1)
    pass_on(3)
    pass_on(0)
    wait(last_recv, gathered.at[pl.ds(0, (n_dp - 1) * tokens)])
    for k in range(SIDE):
        total = gathered[pl.ds(k * SIDE * tokens, tokens)].astype(jnp.float32)
        for j in range(1, SIDE):
            total += gathered[pl.ds((k * SIDE + j) * tokens, tokens)].astype(jnp.float32)
        att_ref[:, pl.ds(k * cols, cols)] = total

    for i, buf in enumerate((keys_own, keys_moved)):
        wait(sends.at[i], buf.at[pl.ds(0, 3 * shard_rows + 4 * shard_rows)])
    wait(sends.at[2], keys_own.at[pl.ds(0, prefix_part - piece)])
    wait(sends.at[3], keys_own.at[pl.ds(0, (n_dp - 1) * new_part)])
    wait(sends.at[4], proj.at[pl.ds(0, 3 * col_part)])
    wait(sends.at[5], keys_own.at[pl.ds(0, prefix_part - piece)])
    for i in range(pairs):
        wait(sends.at[6 + i], heads.at[0, pl.ds(0, 3 * home * 2 // head_count)])
    wait(sends.at[6 + pairs], heads.at[0, pl.ds(0, 3 * late)])
    wait(sends.at[11], summed)
    wait(sends.at[12], summed.at[pl.ds(0, (n_dp - 1) * tokens)])


def attention(queries, prefix_latents, new_latents, lengths, sources, value_up, out_proj, owner):
    span, head_count, key_width = queries.shape
    _, lat, vh = value_up.shape
    n_dp, n_ep = lax.axis_size("dp"), lax.axis_size("ep")
    late = span // 4
    home = span - late
    prefix_part, new_part = prefix_latents.shape[1], new_latents.shape[1]
    key_rows = (prefix_part + new_part) * n_ep
    rows, col_part = out_proj.shape
    cols = col_part * SIDE
    tokens = span // n_ep
    vmem = pl.BlockSpec(memory_space=pltpu.VMEM)
    smem = pl.BlockSpec(memory_space=pltpu.SMEM)
    hbm = pl.BlockSpec(memory_space=pl.ANY)
    bf16, f32 = jnp.bfloat16, jnp.float32
    return pl.pallas_call(
        attention_kernel,
        out_shape=(
            jax.ShapeDtypeStruct((tokens, cols * SIDE), f32),
            jax.ShapeDtypeStruct(new_latents.shape, bf16),
        ),
        in_specs=[smem] * 3 + [vmem] * 3 + [hbm] * 2,
        out_specs=(vmem, vmem),
        scratch_shapes=[
            pltpu.VMEM((head_count, key_width, span), bf16),
            pltpu.VMEM(value_up.shape, bf16),
            pltpu.VMEM((head_count // 2, 2 * home, key_width), bf16),
            pltpu.VMEM((head_count * late, key_width), bf16),
            pltpu.VMEM((key_rows, key_width), bf16),
            pltpu.VMEM((key_rows, key_width), bf16),
            pltpu.VMEM((n_dp, prefix_part // n_dp, key_width), bf16),
            pltpu.VMEM((n_dp, prefix_part // n_dp, key_width), bf16),
            pltpu.VMEM((n_dp, new_part, key_width), bf16),
            pltpu.VMEM((cols, rows), bf16),
            pltpu.VMEM((SIDE, span, rows), bf16),
            pltpu.VMEM((SIDE, span, cols), f32),
            pltpu.VMEM((SIDE, span, cols), bf16),
            pltpu.VMEM((SIDE, SIDE * tokens, cols), bf16),
            pltpu.VMEM((n_dp * tokens, cols), bf16),
            pltpu.VMEM((n_dp * tokens, cols), bf16),
            pltpu.SemaphoreType.DMA((2, 10)),
            pltpu.SemaphoreType.DMA((6,)),
            pltpu.SemaphoreType.DMA((3,)),
            pltpu.SemaphoreType.DMA((5,)),
            pltpu.SemaphoreType.DMA((SIDE,)),
            pltpu.SemaphoreType.DMA,
            pltpu.SemaphoreType.DMA((13,)),
            pltpu.SemaphoreType.DMA((2,)),
        ],
        compiler_params=pltpu.CompilerParams(
            collective_id=2, has_side_effects=True, vmem_limit_bytes=60 * 2**20
        ),
        name="attention",
    )(
        lengths,
        sources,
        owner,
        prefix_latents.transpose(0, 2, 1),
        new_latents,
        out_proj.T,
        queries.transpose(1, 2, 0),
        value_up,
    )


def shards(
    queries,
    prefix_latents,
    new_latents,
    prefix_lengths,
    span_sources,
    value_up,
    out_proj,
    residual,
    norm_gain,
    expert_gate,
    expert_up,
    expert_down,
    expert_ids,
    gate_weights,
    decode_owner,
):
    attention_sum, decode_latents = attention(
        queries,
        prefix_latents,
        new_latents,
        prefix_lengths,
        span_sources,
        value_up,
        out_proj,
        decode_owner,
    )
    layer_out = moe(
        attention_sum,
        residual,
        norm_gain,
        expert_ids,
        gate_weights,
        expert_gate,
        expert_up,
        expert_down,
    )
    return (layer_out, decode_latents)


def solution(mesh):
    return jax.shard_map(
        shards,
        mesh=mesh,
        in_specs=(
            P("dp", "ep", None),
            P("dp", "ep", None),
            P("dp", "ep", None),
            P(),
            P(),
            P("ep", None, None),
            P("ep", "dp"),
            P(("dp", "ep"), None),
            P(),
            P(("dp", "ep"), None, None),
            P(("dp", "ep"), None, None),
            P(("dp", "ep"), None, None),
            P(("dp", "ep"), None),
            P(("dp", "ep"), None),
            P(),
        ),
        out_specs=(P(("dp", "ep"), None), P("dp", "ep", None)),
        check_vma=False,
    )
```

```python
import functools
import math

import jax
import jax.numpy as jnp
from jax import lax
from jax.experimental import pallas as pl
from jax.experimental.pallas import tpu as pltpu
from jax.sharding import PartitionSpec as P

TOP = 8


score_scale = 192.0 ** (-0.5)
exp2_scale = score_scale * math.log2(math.e)
norm_eps = 1e-06


MESH = pl.DeviceIdType.MESH


def partners(count, me, each):
    def step(k, carry):
        each(lax.rem(me + k, count))
        return carry

    lax.fori_loop(1, count, step, 0)


def block_rows(start, size):
    return pl.ds(pl.multiple_of(start * size, size), size)


def moe_kernel(
    sizes,
    att_ref,
    res_ref,
    gain_ref,
    ids_ref,
    gates_ref,
    gate_hbm,
    up_hbm,
    down_hbm,
    out_ref,
    w_gate,
    w_up,
    w_down,
    hid,
    s1,
    r1,
    s2,
    r2,
    total,
    act,
    o1,
    q1,
    q2,
    q3,
    send_sems,
    recv_sems,
    weight_sems,
):
    n_dp, n_ep, chunks = sizes
    dp, ep = lax.axis_index("dp"), lax.axis_index("ep")
    rows = n_dp * n_ep * 2
    dp_block, ep_block = 2 * n_ep, 2 * n_dp
    cols = hid.shape[1] // chunks
    tokens = hid.shape[0]
    hidden_units = w_gate.shape[1]

    loads = [
        pltpu.make_async_copy(src.at[0], dst, weight_sems.at[i])
        for i, (src, dst) in enumerate(((gate_hbm, w_gate), (up_hbm, w_up), (down_hbm, w_down)))
    ]
    for load in loads:
        load.start()

    barrier = pltpu.get_barrier_semaphore()
    partners(
        n_dp,
        dp,
        lambda p: pl.semaphore_signal(barrier, inc=1, device_id=(p, ep), device_id_type=MESH),
    )
    partners(
        n_ep,
        ep,
        lambda p: pl.semaphore_signal(barrier, inc=1, device_id=(dp, p), device_id_type=MESH),
    )

    def send_dp(stage, c, src, dst):
        def each(p):
            pltpu.make_async_remote_copy(
                src_ref=src.at[c, block_rows(p, dp_block)],
                dst_ref=dst.at[c, block_rows(dp, dp_block)],
                send_sem=send_sems.at[stage, c],
                recv_sem=recv_sems.at[stage, c],
                device_id=(p, ep),
                device_id_type=MESH,
            ).start()

        partners(n_dp, dp, each)
        dst[c, block_rows(dp, dp_block)] = src[c, block_rows(dp, dp_block)]


    def send_ep(stage, c, src, dst):
        def each(p):
            pltpu.make_async_remote_copy(
                src_ref=src.at[c, block_rows(p, ep_block)],
                dst_ref=dst.at[c, block_rows(ep, ep_block)],
                send_sem=send_sems.at[stage, c],
                recv_sem=recv_sems.at[stage, c],
                device_id=(dp, p),
                device_id_type=MESH,
            ).start()

        partners(n_ep, ep, each)
        dst[c, block_rows(ep, ep_block)] = src[c, block_rows(ep, ep_block)]

    def over_dp(stage, c):
        return (c % 2 == 0) == (stage in (0, 3))

    def hop(stage, c, src, dst):
        (send_dp if over_dp(stage, c) else send_ep)(stage, c, src, dst)

    def wait_all(sems, stage, c, ref):
        size = rows - (dp_block if over_dp(stage, c) else ep_block)
        part = ref.at[c, pl.ds(0, size)]
        pltpu.make_async_copy(part, part, sems.at[stage, c]).wait()

    def mm(a, b):
        return jnp.dot(a, b, preferred_element_type=jnp.float32)

    slot = lax.broadcasted_iota(jnp.int32, (rows, tokens), 0)
    named = jnp.zeros((rows, tokens), jnp.float32)
    weight = jnp.zeros((rows, tokens), jnp.float32)
    for k in range(TOP):
        hit = ids_ref[k : k + 1, :] == (slot >> 1)
        named += jnp.where(hit, 1.0, 0.0)
        weight += jnp.where(hit, gates_ref[k : k + 1, :], 0.0)
    first = lax.broadcasted_iota(jnp.int32, (tokens, tokens), 0)
    second = lax.broadcasted_iota(jnp.int32, (tokens, tokens), 1)
    before = jnp.where(first < second, 1.0, 0.0).astype(jnp.bfloat16)
    same = jnp.where(first == second, 1.0, 0.0).astype(jnp.bfloat16)
    chosen = mm(named.astype(jnp.bfloat16), before) == (slot & 1).astype(jnp.float32)
    pick = jnp.where(chosen, named, 0.0).astype(jnp.bfloat16)
    weight = jnp.where(chosen, weight, 0.0)
    weight_high = weight.astype(jnp.bfloat16)
    weight_low = (weight - weight_high.astype(jnp.float32)).astype(jnp.bfloat16)
    weight_high = contract_last(same, weight_high).astype(jnp.bfloat16)
    weight_low = contract_last(same, weight_low).astype(jnp.bfloat16)
    weights = jnp.concatenate([weight_high, weight_low], axis=0)
    to = lax.broadcasted_iota(jnp.int32, (rows, rows), 0)
    frm = lax.broadcasted_iota(jnp.int32, (rows, rows), 1)
    by_ep = lax.rem(to >> 1, n_dp) * dp_block + (to // ep_block) * 2 + (to & 1)
    by_dp = lax.rem(to >> 1, n_ep) * ep_block + (to // dp_block) * 2 + (to & 1)
    perm_ep = jnp.where(frm == by_ep, 1.0, 0.0).astype(jnp.bfloat16)
    perm_dp = jnp.where(frm == by_dp, 1.0, 0.0).astype(jnp.bfloat16)
    picks = (pick, mm(perm_ep, pick).astype(jnp.bfloat16))
    weights = (weights, contract_last(weights, perm_ep).astype(jnp.bfloat16))
    perms = (perm_ep, perm_dp)

    hidden = res_ref[...].astype(jnp.float32) + att_ref[...].astype(jnp.float32)
    hid[...] = hidden
    mean_square = jnp.mean(hidden * hidden, axis=1, keepdims=True)
    scale = lax.rsqrt(mean_square + norm_eps)

    pl.semaphore_wait(barrier, n_dp + n_ep - 2)

    for c in range(chunks):
        span = pl.ds(c * cols, cols)
        normed = (hid[:, span] * scale * gain_ref[:, span].astype(jnp.float32)).astype(
            jnp.bfloat16
        )
        s1[c] = mm(picks[c % 2], normed).astype(jnp.bfloat16)
        hop(0, c, s1, r1)
    for c in range(chunks):
        wait_all(recv_sems, 0, c, r1)
        s2[c] = mm(perms[c % 2], r1[c]).astype(jnp.bfloat16)
        hop(1, c, s2, r2)
    loads[0].wait()
    loads[1].wait()
    for c in range(chunks):
        wait_all(recv_sems, 1, c, r2)
        span = pl.ds(c * cols, cols)
        x = r2[c]
        if c % 2:
            x = mm(perm_ep, x).astype(jnp.bfloat16)
        gate_part = mm(x, w_gate[span, :])
        up_part = mm(x, w_up[span, :])
        if c:
            gate_part += total[:, pl.ds(0, hidden_units)]
            up_part += total[:, pl.ds(hidden_units, hidden_units)]
        if c < chunks - 1:
            total[:, pl.ds(0, hidden_units)] = gate_part
            total[:, pl.ds(hidden_units, hidden_units)] = up_part
        else:
            act[0] = (gate_part / (1.0 + jnp.exp(-gate_part)) * up_part).astype(jnp.bfloat16)
    act[1] = mm(perm_dp, act[0]).astype(jnp.bfloat16)
    loads[2].wait()
    for c in range(chunks):
        o1[c] = mm(act[c % 2], w_down[:, pl.ds(c * cols, cols)]).astype(jnp.bfloat16)
        hop(2, c, o1, q1)
    for c in range(chunks):
        wait_all(recv_sems, 2, c, q1)
        q2[c] = mm(perms[1 - c % 2], q1[c]).astype(jnp.bfloat16)
        hop(3, c, q2, q3)
    for c in range(chunks):
        wait_all(recv_sems, 3, c, q3)
        span = pl.ds(c * cols, cols)
        both = mm(weights[c % 2], q3[c])
        out_ref[:, span] = (hid[:, span] + (both[:tokens] + both[tokens:])).astype(out_ref.dtype)
    for stage, ref in enumerate((s1, s2, o1, q2)):
        for c in range(chunks):
            wait_all(send_sems, stage, c, ref)


def moe(attention, residual, norm_gain, expert_ids, gate_weights, expert_gate, expert_up, expert_down):
    n_dp, n_ep = lax.axis_size("dp"), lax.axis_size("ep")
    tokens, width = residual.shape
    units = expert_gate.shape[2]
    rows = n_dp * n_ep * 2
    chunks = 4
    buf = pltpu.VMEM((chunks, rows, width // chunks), jnp.bfloat16)
    vmem = pl.BlockSpec(memory_space=pltpu.VMEM)
    hbm = pl.BlockSpec(memory_space=pl.ANY)
    return pl.pallas_call(
        functools.partial(moe_kernel, (n_dp, n_ep, chunks)),
        out_shape=jax.ShapeDtypeStruct((tokens, width), jnp.bfloat16),
        in_specs=[vmem] * 5 + [hbm] * 3,
        out_specs=vmem,
        scratch_shapes=[
            pltpu.VMEM((width, units), jnp.bfloat16),
            pltpu.VMEM((width, units), jnp.bfloat16),
            pltpu.VMEM((units, width), jnp.bfloat16),
            pltpu.VMEM((tokens, width), jnp.float32),
            buf,
            buf,
            buf,
            buf,
            pltpu.VMEM((rows, 2 * units), jnp.float32),
            pltpu.VMEM((2, rows, units), jnp.bfloat16),
            buf,
            buf,
            buf,
            buf,
            pltpu.SemaphoreType.DMA((4, chunks)),
            pltpu.SemaphoreType.DMA((4, chunks)),
            pltpu.SemaphoreType.DMA((3,)),
        ],
        compiler_params=pltpu.CompilerParams(
            collective_id=1, has_side_effects=True, vmem_limit_bytes=60 * 2**20
        ),
        name="experts",
    )(
        attention,
        residual,
        norm_gain.reshape(1, -1),
        expert_ids.T,
        gate_weights.T,
        expert_gate,
        expert_up,
        expert_down,
    )


def contract_last(a, b):
    return lax.dot_general(a, b, (((1,), (1,)), ((), ())), preferred_element_type=jnp.float32)


def attend(q, keys, length, positions, prefix_len, lat):
    s_old = contract_last(q, keys[0:prefix_len, :])
    s_new = contract_last(q, keys[prefix_len:, :])
    old_pos = lax.broadcasted_iota(jnp.int32, (1, prefix_len), 1)
    s_old = s_old + jnp.where(old_pos < length, 0.0, -1e30)
    new_pos = lax.broadcasted_iota(jnp.int32, s_new.shape, 1)
    s_new = jnp.where(new_pos <= positions, s_new, -1e30)
    top = jnp.maximum(
        jnp.max(s_old, axis=1, keepdims=True), jnp.max(s_new, axis=1, keepdims=True)
    )
    e_old = jnp.exp2((s_old - top) * exp2_scale)
    e_new = jnp.exp2((s_new - top) * exp2_scale)
    weight_sum = jnp.sum(e_old, axis=1, keepdims=True) + jnp.sum(e_new, axis=1, keepdims=True)
    weighted = jnp.dot(
        e_old.astype(jnp.bfloat16), keys[0:prefix_len, 0:lat], preferred_element_type=jnp.float32
    )
    weighted += jnp.dot(
        e_new.astype(jnp.bfloat16), keys[prefix_len:, 0:lat], preferred_element_type=jnp.float32
    )
    return (weighted * (1.0 / weight_sum)).astype(jnp.bfloat16)


SIDE = 4


def attention_kernel(
    lengths_ref,
    sources_ref,
    owner_ref,
    prefix_ref,
    new_ref,
    proj_ref,
    queries_hbm,
    value_up_hbm,
    att_ref,
    decode_ref,
    q_raw,
    value_up,
    q_home,
    q_late,
    keys_own,
    late_own,
    late_in,
    late_on,
    rows_own,
    rows_in,
    rows_on,
    rows_back,
    news_y,
    news_out,
    news_x,
    proj,
    heads,
    heads_late,
    part,
    part_b,
    pair,
    summed,
    gathered,
    z_recv,
    y_recv,
    dp_recv,
    x_recv,
    pair_recv,
    last_recv,
    sends,
    load_sems,
):
    dp, ep = lax.axis_index("dp"), lax.axis_index("ep")
    x, y = dp // SIDE, lax.rem(dp, SIDE)
    z, core = ep // 2, lax.rem(ep, 2)
    n_dp = SIDE * SIDE
    n_ep = 2 * SIDE
    prefix_part, new_part = prefix_ref.shape[2], new_ref.shape[1]
    prefix_len = prefix_part * n_ep
    shard_rows = prefix_part + new_part
    head_count, lat, vh = value_up.shape
    span = q_raw.shape[2]
    late = span // 4
    home = span - late
    tokens = span // n_ep
    strip = tokens // 2
    block = home // 2
    quad = head_count // 2
    col_part = proj_ref.shape[0]
    cols = col_part * SIDE
    piece = head_count * late // n_dp

    def around(a, k):
        return lax.rem(a + k + SIDE, SIDE)

    def device(x2, y2, z2, core2):
        return (x2 * SIDE + y2, z2 * 2 + core2)

    right_z, left_z = device(x, y, around(z, 1), core), device(x, y, around(z, -1), core)
    right_y, left_y = device(x, around(y, 1), z, core), device(x, around(y, -1), z, core)
    sibling = device(x, y, z, 1 - core)

    load_q = pltpu.make_async_copy(queries_hbm, q_raw, load_sems.at[0])
    load_q.start()
    load_v = pltpu.make_async_copy(value_up_hbm, value_up, load_sems.at[1])
    load_v.start()

    barrier = pltpu.get_barrier_semaphore()

    def hello(to):
        pl.semaphore_signal(barrier, inc=1, device_id=to, device_id_type=MESH)

    partners(n_dp, dp, lambda p: hello((p, ep)))
    for kz in range(1, SIDE):
        for kx in range(SIDE):
            hello(device(around(x, kx), y, around(z, kz), core))
    hello(sibling)

    def send(src, dst, to, send_sem, recv_sem):
        pltpu.make_async_remote_copy(
            src_ref=src,
            dst_ref=dst,
            send_sem=send_sem,
            recv_sem=recv_sem,
            device_id=to,
            device_id_type=MESH,
        ).start()

    def wait(sem, ref):
        pltpu.make_async_copy(ref, ref, sem).wait()

    def key_parts(buf, z2, core2, half):
        at = z2 * 2 + core2
        n, m = (prefix_part // 2, new_part // 2) if half is not None else (prefix_part, new_part)
        half = half or 0
        old = pl.multiple_of(at * prefix_part + half * n, n)
        new = pl.multiple_of(prefix_len + at * new_part + half * m, m)
        return [buf.at[pl.ds(old, n)], buf.at[pl.ds(new, m)]]

    eye_a = lax.broadcasted_iota(jnp.int32, (span, span), 0)
    eye_b = lax.broadcasted_iota(jnp.int32, (span, span), 1)
    eye = jnp.where(eye_a == eye_b, 1.0, 0.0).astype(jnp.bfloat16)
    keys_own[block_rows(ep, prefix_part)] = contract_last(eye, prefix_ref[0]).astype(jnp.bfloat16)
    keys_own[pl.ds(pl.multiple_of(prefix_len + ep * new_part, new_part), new_part)] = new_ref[0]
    proj[block_rows(y, col_part)] = proj_ref[...]

    pl.semaphore_wait(barrier, n_dp - 1 + (SIDE - 1) * SIDE + 1)

    def ring_start(refs, right, left, send_sem, recv):
        for half in (0, 1):
            for ref in refs(0, half):
                send(ref, ref, right, send_sem, recv.at[half])
            for ref in refs(0, 1 - half):
                send(ref, ref, left, send_sem, recv.at[2 + 1 - half])

    def ring_forward(refs, right, left, send_sem, recv, half_ref):
        wait(recv.at[0], half_ref)
        for ref in refs(-1, 0):
            send(ref, ref, right, send_sem, recv.at[4])
        wait(recv.at[3], half_ref)
        for ref in refs(1, 1):
            send(ref, ref, left, send_sem, recv.at[5])

    key_half = keys_own.at[pl.ds(0, shard_rows // 2)]
    key_full = keys_own.at[pl.ds(0, shard_rows)]

    def key_refs(k, half):
        return key_parts(keys_own, around(z, k), core, half)

    def share(k, sem):
        for ref in key_refs(k, None):
            send(ref, ref, sibling, sends.at[0], z_recv.at[sem])

    def everywhere(src, dst, send_sem, recv_sem):
        partners(n_dp, dp, lambda p: send(src(p), dst, (p, ep), send_sem, recv_sem))

    ring_start(key_refs, right_z, left_z, sends.at[0], z_recv)
    share(0, 6)

    def over_axis(along_x, src, dst, send_sem, recv_sem):
        for k in (2, 1, 3):
            to = device(around(x, k), y, z, core) if along_x else device(x, around(y, k), z, core)
            send(src(k), dst, to, send_sem, recv_sem)

    def proj_refs(k, half):
        n = col_part // 2
        start = pl.multiple_of(around(y, k) * col_part + half * n, n)
        return [proj.at[pl.ds(start, n)]]

    load_q.wait()
    for h in range(head_count):
        rows = contract_last(eye, q_raw[h]).astype(jnp.bfloat16)
        late_own[pl.ds(h * late, late)] = rows[home:]
        for b in range(2):
            for e in range(home // tokens):
                at = (h % quad) * block + (e % 2) * block // 2 + (e // 2) * strip
                row = e * tokens + b * strip
                q_home[2 * b + h // quad, pl.ds(at, strip)] = rows[row : row + strip]
    all_late = keys_own.at[pl.ds(0, (n_dp - 1) * piece)]
    all_rows = rows_own.at[pl.ds(0, (n_dp - 1) * piece)]
    everywhere(
        lambda p: late_own.at[block_rows(p, piece)], late_in.at[dp], sends.at[1], dp_recv.at[0]
    )
    late_in[dp] = late_own[block_rows(dp, piece)]
    all_news = keys_own.at[pl.ds(0, (SIDE - 1) * new_part)]
    news_y[y] = new_ref[0]
    over_axis(False, lambda k: news_y.at[y], news_y.at[y], sends.at[3], dp_recv.at[1])
    ring_forward(key_refs, right_z, left_z, sends.at[0], z_recv, key_half)
    wait(z_recv.at[1], key_half)
    share(-1, 7)
    wait(z_recv.at[2], key_half)
    share(1, 8)
    wait(dp_recv.at[0], all_late)

    def stage_late(i, carry):
        slot = jnp.int32(0)
        for s in range(n_dp):
            slot = jnp.maximum(slot, jnp.where(sources_ref[s] == i, s, 0))
        late_on[i] = late_in[slot]
        return carry

    lax.fori_loop(0, n_dp, stage_late, 0)
    everywhere(
        lambda p: late_on.at[p], q_late.at[block_rows(dp, piece)], sends.at[2], dp_recv.at[2]
    )
    q_late[block_rows(dp, piece)] = late_on[dp]
    ring_start(proj_refs, right_y, left_y, sends.at[4], y_recv)
    wait(z_recv.at[4], key_half)
    wait(z_recv.at[5], key_half)
    share(2, 9)
    load_v.wait()
    for sem in range(6, 10):
        wait(z_recv.at[sem], key_full)

    def given_to(slot):
        given = jnp.int32(0)
        for i in range(n_dp):
            given = jnp.maximum(given, jnp.where(owner_ref[i] == slot, i, 0))
        return given

    def send_heads(i, refs):
        for ref in refs:
            over_axis(True, lambda k: ref, ref, sends.at[6 + i], x_recv.at[i])

    row = lax.broadcasted_iota(jnp.int32, (quad * block, 1), 0)
    within = row
    for j in range(1, quad):
        within -= jnp.where(row >= j * block, block, 0)
    on_core = jnp.where(within >= block // 2, 1, 0)
    within -= on_core * (block // 2)
    home_pos = ((within // strip) * 2 + on_core) * tokens + lax.rem(within, strip)
    half_rows = SIDE * block // 2

    def home_part(b, half):
        positions = home_pos + b * strip
        out = attend(q_home[2 * b + half], keys_own, lengths_ref[dp], positions, prefix_len, lat)
        for j in range(quad):
            h = half * quad + j
            rows = jnp.dot(
                out[j * block : (j + 1) * block], value_up[h], preferred_element_type=jnp.float32
            ).astype(jnp.bfloat16)
            for c in range(2):
                at = pl.multiple_of(c * half_rows + x * (block // 2), block // 2)
                heads[b, pl.ds(at, block // 2), pl.ds(h * vh, vh)] = rows[
                    c * block // 2 : (c + 1) * block // 2
                ]
        refs = []
        for c in range(2):
            at = pl.multiple_of(c * half_rows + x * (block // 2), block // 2)
            refs.append(
                heads.at[b, pl.ds(at, block // 2), pl.ds(half * quad * vh, quad * vh)]
            )
        send_heads(2 * b + half, refs)

    def wait_heads(i):
        wait(x_recv.at[i], heads.at[0, pl.ds(0, (SIDE - 1) * block // 2)])

    def project(i, rows):
        n = rows.shape[0]
        out = contract_last(rows, proj[...])
        part[i, pl.ds(0, n)] = out
        part_b[i, pl.ds(0, n)] = out.astype(jnp.bfloat16)
        other = part_b.at[i, pl.ds(pl.multiple_of((1 - core) * (n // 2), n // 2), n // 2)]
        send(other, pair.at[i, pl.ds(0, n // 2)], sibling, sends.at[11 + i], pair_recv.at[i])

    def pass_on(i, n, to_z, size, offset):
        wait(pair_recv.at[i], pair.at[i, pl.ds(0, n // 2)])
        mine = part[i, pl.ds(pl.multiple_of(core * (n // 2), n // 2), n // 2)]
        both = mine + pair[i, pl.ds(0, n // 2)].astype(jnp.float32)
        summed[i, pl.ds(0, n // 2)] = both.astype(jnp.bfloat16)
        start = (x * SIDE + z) * tokens + offset
        landing = pl.ds(pl.multiple_of(start, size), size)
        for k in (2, 1, 3, 0):
            xk = around(x, k)
            for j, zk in enumerate(to_z):
                at = pl.multiple_of((xk * len(to_z) + j) * size, size)

                def go():
                    send(
                        summed.at[i, pl.ds(at, size)],
                        gathered.at[landing],
                        device(xk, y, zk, core),
                        sends.at[14],
                        last_recv,
                    )

                if k:
                    go()
                else:
                    pl.when(z != zk)(go)

                    @pl.when(z == zk)
                    def _():
                        gathered[landing] = summed[i, pl.ds(at, size)]

    home_part(0, 0)
    wait(dp_recv.at[1], all_news)
    for k in range(SIDE):
        slot = around(x, k) * SIDE + y
        news_out[k] = news_y[lax.rem(given_to(slot), SIDE)]
    over_axis(True, lambda k: news_out.at[k], news_x.at[x], sends.at[15], dp_recv.at[5])
    news_x[x] = news_out[0]
    home_part(0, 1)
    proj_half = proj.at[pl.ds(0, col_part // 2)]
    ring_forward(proj_refs, right_y, left_y, sends.at[4], y_recv, proj_half)
    wait(dp_recv.at[2], all_late)
    late_row = lax.broadcasted_iota(jnp.int32, (head_count * late, 1), 0)
    late_pos = lax.rem(late_row, late) + home
    out = attend(q_late[...], keys_own, lengths_ref[dp], late_pos, prefix_len, lat)
    for h in range(head_count):
        rows_own[pl.ds(h * late, late)] = jnp.dot(
            out[h * late : (h + 1) * late], value_up[h], preferred_element_type=jnp.float32
        ).astype(jnp.bfloat16)
    everywhere(
        lambda p: rows_own.at[block_rows(p, piece)], rows_in.at[dp], sends.at[5], dp_recv.at[3]
    )
    rows_in[dp] = rows_own[block_rows(dp, piece)]
    home_part(1, 0)
    wait(dp_recv.at[3], all_rows)

    def stage_rows(s, carry):
        rows_on[s] = rows_in[sources_ref[s]]
        return carry

    lax.fori_loop(0, n_dp, stage_rows, 0)
    everywhere(
        lambda p: rows_on.at[p], rows_back.at[block_rows(dp, piece)], sends.at[16], dp_recv.at[4]
    )
    rows_back[block_rows(dp, piece)] = rows_on[dp]
    for i in (1, 2, 4, 5):
        wait(y_recv.at[i], proj_half)
    wait_heads(0)
    wait_heads(1)
    project(0, heads[0])
    home_part(1, 1)
    wait(dp_recv.at[4], all_rows)
    late_part = late // 2
    refs = []
    for c in range(2):
        at = pl.multiple_of(c * SIDE * late_part + x * late_part, late_part)
        refs.append(heads_late.at[pl.ds(at, late_part)])
        for h in range(head_count):
            heads_late[pl.ds(at, late_part), pl.ds(h * vh, vh)] = rows_back[
                pl.ds(h * late + c * late_part, late_part)
            ]
    send_heads(4, refs)
    home_z = tuple(range(home // tokens // 2))
    late_z = (SIDE - 1,)
    home_rows, late_rows = SIDE * block, SIDE * late
    pass_on(0, home_rows, home_z, strip, 0)
    wait_heads(2)
    wait_heads(3)
    project(1, heads[1])
    wait(x_recv.at[4], heads_late.at[pl.ds(0, (SIDE - 1) * late)])
    project(2, heads_late[...])
    pass_on(1, home_rows, home_z, strip, strip)
    pass_on(2, late_rows, late_z, tokens, 0)
    wait(dp_recv.at[5], all_news)
    decode_ref[0] = news_x[given_to(dp) // SIDE]
    wait(last_recv, gathered.at[pl.ds(0, (n_dp - 1) * tokens)])
    for k in range(SIDE):
        total = gathered[pl.ds(k * SIDE * tokens, tokens)].astype(jnp.float32)
        for j in range(1, SIDE):
            total += gathered[pl.ds((k * SIDE + j) * tokens, tokens)].astype(jnp.float32)
        att_ref[:, pl.ds(k * cols, cols)] = total

    wait(sends.at[0], keys_own.at[pl.ds(0, 3 * shard_rows + 4 * shard_rows)])
    wait(sends.at[1], all_late)
    wait(sends.at[2], all_late)
    wait(sends.at[3], all_news)
    wait(sends.at[15], all_news)
    wait(sends.at[4], proj.at[pl.ds(0, 3 * col_part)])
    wait(sends.at[5], all_rows)
    wait(sends.at[16], all_rows)
    for i in range(4):
        wait(sends.at[6 + i], heads.at[0, pl.ds(0, (SIDE - 1) * block // 2)])
    wait(sends.at[10], heads_late.at[pl.ds(0, (SIDE - 1) * late)])
    for i in range(2):
        wait(sends.at[11 + i], pair.at[i])
    wait(sends.at[13], pair.at[2, pl.ds(0, late_rows // 2)])
    wait(sends.at[14], gathered.at[pl.ds(0, (n_dp - 1) * tokens)])


def attention(queries, prefix_latents, new_latents, lengths, sources, value_up, out_proj, owner):
    span, head_count, key_width = queries.shape
    _, lat, vh = value_up.shape
    n_dp, n_ep = lax.axis_size("dp"), lax.axis_size("ep")
    late = span // 4
    home = span - late
    late_rows = head_count * late
    prefix_part, new_part = prefix_latents.shape[1], new_latents.shape[1]
    key_rows = (prefix_part + new_part) * n_ep
    rows, col_part = out_proj.shape
    cols = col_part * SIDE
    tokens = span // n_ep
    vmem = pl.BlockSpec(memory_space=pltpu.VMEM)
    smem = pl.BlockSpec(memory_space=pltpu.SMEM)
    hbm = pl.BlockSpec(memory_space=pl.ANY)
    bf16, f32 = jnp.bfloat16, jnp.float32
    return pl.pallas_call(
        attention_kernel,
        out_shape=(
            jax.ShapeDtypeStruct((tokens, cols * SIDE), f32),
            jax.ShapeDtypeStruct(new_latents.shape, bf16),
        ),
        in_specs=[smem] * 3 + [vmem] * 3 + [hbm] * 2,
        out_specs=(vmem, vmem),
        scratch_shapes=[
            pltpu.VMEM((head_count, key_width, span), bf16),
            pltpu.VMEM(value_up.shape, bf16),
            pltpu.VMEM((4, head_count // 2 * (home // 2), key_width), bf16),
            pltpu.VMEM((late_rows, key_width), bf16),
            pltpu.VMEM((key_rows, key_width), bf16),
            pltpu.VMEM((late_rows, key_width), bf16),
            pltpu.VMEM((n_dp, late_rows // n_dp, key_width), bf16),
            pltpu.VMEM((n_dp, late_rows // n_dp, key_width), bf16),
            pltpu.VMEM((late_rows, vh), bf16),
            pltpu.VMEM((n_dp, late_rows // n_dp, vh), bf16),
            pltpu.VMEM((n_dp, late_rows // n_dp, vh), bf16),
            pltpu.VMEM((late_rows, vh), bf16),
            pltpu.VMEM((SIDE, new_part, key_width), bf16),
            pltpu.VMEM((SIDE, new_part, key_width), bf16),
            pltpu.VMEM((SIDE, new_part, key_width), bf16),
            pltpu.VMEM((cols, rows), bf16),
            pltpu.VMEM((2, SIDE * home // 2, rows), bf16),
            pltpu.VMEM((SIDE * late, rows), bf16),
            pltpu.VMEM((3, SIDE * home // 2, cols), f32),
            pltpu.VMEM((3, SIDE * home // 2, cols), bf16),
            pltpu.VMEM((3, SIDE * home // 4, cols), bf16),
            pltpu.VMEM((3, SIDE * home // 4, cols), bf16),
            pltpu.VMEM((n_dp * tokens, cols), bf16),
            pltpu.SemaphoreType.DMA((10,)),
            pltpu.SemaphoreType.DMA((6,)),
            pltpu.SemaphoreType.DMA((6,)),
            pltpu.SemaphoreType.DMA((5,)),
            pltpu.SemaphoreType.DMA((3,)),
            pltpu.SemaphoreType.DMA,
            pltpu.SemaphoreType.DMA((17,)),
            pltpu.SemaphoreType.DMA((2,)),
        ],
        compiler_params=pltpu.CompilerParams(
            collective_id=2, has_side_effects=True, vmem_limit_bytes=60 * 2**20
        ),
        name="attention",
    )(
        lengths,
        sources,
        owner,
        prefix_latents.transpose(0, 2, 1),
        new_latents,
        out_proj.T,
        queries.transpose(1, 2, 0),
        value_up,
    )


def shards(
    queries,
    prefix_latents,
    new_latents,
    prefix_lengths,
    span_sources,
    value_up,
    out_proj,
    residual,
    norm_gain,
    expert_gate,
    expert_up,
    expert_down,
    expert_ids,
    gate_weights,
    decode_owner,
):
    attention_sum, decode_latents = attention(
        queries,
        prefix_latents,
        new_latents,
        prefix_lengths,
        span_sources,
        value_up,
        out_proj,
        decode_owner,
    )
    layer_out = moe(
        attention_sum,
        residual,
        norm_gain,
        expert_ids,
        gate_weights,
        expert_gate,
        expert_up,
        expert_down,
    )
    return (layer_out, decode_latents)


def solution(mesh):
    return jax.shard_map(
        shards,
        mesh=mesh,
        in_specs=(
            P("dp", "ep", None),
            P("dp", "ep", None),
            P("dp", "ep", None),
            P(),
            P(),
            P("ep", None, None),
            P("ep", "dp"),
            P(("dp", "ep"), None),
            P(),
            P(("dp", "ep"), None, None),
            P(("dp", "ep"), None, None),
            P(("dp", "ep"), None, None),
            P(("dp", "ep"), None),
            P(("dp", "ep"), None),
            P(),
        ),
        out_specs=(P(("dp", "ep"), None), P("dp", "ep", None)),
        check_vma=False,
    )
```

```python
import functools
import math

import jax
import jax.numpy as jnp
from jax import lax
from jax.experimental import pallas as pl
from jax.experimental.pallas import tpu as pltpu
from jax.sharding import PartitionSpec as P

TOP = 8


score_scale = 192.0 ** (-0.5)
exp2_scale = score_scale * math.log2(math.e)
norm_eps = 1e-06


MESH = pl.DeviceIdType.MESH


def partners(count, me, each):
    def step(k, carry):
        each(lax.rem(me + k, count))
        return carry

    lax.fori_loop(1, count, step, 0)


def block_rows(start, size):
    return pl.ds(pl.multiple_of(start * size, size), size)


def moe_kernel(
    sizes,
    att_ref,
    res_ref,
    gain_ref,
    ids_ref,
    gates_ref,
    gate_hbm,
    up_hbm,
    down_hbm,
    out_ref,
    w_gate,
    w_up,
    w_down,
    hid,
    s1,
    r1,
    s2,
    r2,
    total,
    act,
    o1,
    q1,
    q2,
    q3,
    send_sems,
    recv_sems,
    weight_sems,
):
    n_dp, n_ep, chunks = sizes
    dp, ep = lax.axis_index("dp"), lax.axis_index("ep")
    rows = n_dp * n_ep * 2
    dp_block, ep_block = 2 * n_ep, 2 * n_dp
    cols = hid.shape[1] // chunks
    tokens = hid.shape[0]
    hidden_units = w_gate.shape[1]

    loads = [
        pltpu.make_async_copy(src.at[0], dst, weight_sems.at[i])
        for i, (src, dst) in enumerate(((gate_hbm, w_gate), (up_hbm, w_up), (down_hbm, w_down)))
    ]
    for load in loads:
        load.start()

    barrier = pltpu.get_barrier_semaphore()
    partners(
        n_dp,
        dp,
        lambda p: pl.semaphore_signal(barrier, inc=1, device_id=(p, ep), device_id_type=MESH),
    )
    partners(
        n_ep,
        ep,
        lambda p: pl.semaphore_signal(barrier, inc=1, device_id=(dp, p), device_id_type=MESH),
    )

    def send_dp(stage, c, src, dst):
        def each(p):
            pltpu.make_async_remote_copy(
                src_ref=src.at[c, block_rows(p, dp_block)],
                dst_ref=dst.at[c, block_rows(dp, dp_block)],
                send_sem=send_sems.at[stage, c],
                recv_sem=recv_sems.at[stage, c],
                device_id=(p, ep),
                device_id_type=MESH,
            ).start()

        partners(n_dp, dp, each)
        dst[c, block_rows(dp, dp_block)] = src[c, block_rows(dp, dp_block)]


    def send_ep(stage, c, src, dst):
        def each(p):
            pltpu.make_async_remote_copy(
                src_ref=src.at[c, block_rows(p, ep_block)],
                dst_ref=dst.at[c, block_rows(ep, ep_block)],
                send_sem=send_sems.at[stage, c],
                recv_sem=recv_sems.at[stage, c],
                device_id=(dp, p),
                device_id_type=MESH,
            ).start()

        partners(n_ep, ep, each)
        dst[c, block_rows(ep, ep_block)] = src[c, block_rows(ep, ep_block)]

    def over_dp(stage, c):
        return (c % 2 == 0) == (stage in (0, 3))

    def hop(stage, c, src, dst):
        (send_dp if over_dp(stage, c) else send_ep)(stage, c, src, dst)

    def wait_all(sems, stage, c, ref):
        size = rows - (dp_block if over_dp(stage, c) else ep_block)
        part = ref.at[c, pl.ds(0, size)]
        pltpu.make_async_copy(part, part, sems.at[stage, c]).wait()

    def mm(a, b):
        return jnp.dot(a, b, preferred_element_type=jnp.float32)

    slot = lax.broadcasted_iota(jnp.int32, (rows, tokens), 0)
    named = jnp.zeros((rows, tokens), jnp.float32)
    weight = jnp.zeros((rows, tokens), jnp.float32)
    for k in range(TOP):
        hit = ids_ref[k : k + 1, :] == (slot >> 1)
        named += jnp.where(hit, 1.0, 0.0)
        weight += jnp.where(hit, gates_ref[k : k + 1, :], 0.0)
    first = lax.broadcasted_iota(jnp.int32, (tokens, tokens), 0)
    second = lax.broadcasted_iota(jnp.int32, (tokens, tokens), 1)
    before = jnp.where(first < second, 1.0, 0.0).astype(jnp.bfloat16)
    same = jnp.where(first == second, 1.0, 0.0).astype(jnp.bfloat16)
    chosen = mm(named.astype(jnp.bfloat16), before) == (slot & 1).astype(jnp.float32)
    pick = jnp.where(chosen, named, 0.0).astype(jnp.bfloat16)
    weight = jnp.where(chosen, weight, 0.0)
    weight_high = weight.astype(jnp.bfloat16)
    weight_low = (weight - weight_high.astype(jnp.float32)).astype(jnp.bfloat16)
    weight_high = contract_last(same, weight_high).astype(jnp.bfloat16)
    weight_low = contract_last(same, weight_low).astype(jnp.bfloat16)
    weights = jnp.concatenate([weight_high, weight_low], axis=0)
    to = lax.broadcasted_iota(jnp.int32, (rows, rows), 0)
    frm = lax.broadcasted_iota(jnp.int32, (rows, rows), 1)
    by_ep = lax.rem(to >> 1, n_dp) * dp_block + (to // ep_block) * 2 + (to & 1)
    by_dp = lax.rem(to >> 1, n_ep) * ep_block + (to // dp_block) * 2 + (to & 1)
    perm_ep = jnp.where(frm == by_ep, 1.0, 0.0).astype(jnp.bfloat16)
    perm_dp = jnp.where(frm == by_dp, 1.0, 0.0).astype(jnp.bfloat16)
    picks = (pick, mm(perm_ep, pick).astype(jnp.bfloat16))
    weights = (weights, contract_last(weights, perm_ep).astype(jnp.bfloat16))
    perms = (perm_ep, perm_dp)

    hidden = res_ref[...].astype(jnp.float32) + att_ref[...].astype(jnp.float32)
    hid[...] = hidden
    mean_square = jnp.mean(hidden * hidden, axis=1, keepdims=True)
    scale = lax.rsqrt(mean_square + norm_eps)

    pl.semaphore_wait(barrier, n_dp + n_ep - 2)

    for c in range(chunks):
        span = pl.ds(c * cols, cols)
        normed = (hid[:, span] * scale * gain_ref[span].astype(jnp.float32).reshape(1, cols)).astype(
            jnp.bfloat16
        )
        s1[c] = mm(picks[c % 2], normed).astype(jnp.bfloat16)
        hop(0, c, s1, r1)
    for c in range(chunks):
        wait_all(recv_sems, 0, c, r1)
        s2[c] = mm(perms[c % 2], r1[c]).astype(jnp.bfloat16)
        hop(1, c, s2, r2)
    loads[0].wait()
    loads[1].wait()
    for c in range(chunks):
        wait_all(recv_sems, 1, c, r2)
        span = pl.ds(c * cols, cols)
        x = r2[c]
        if c % 2:
            x = mm(perm_ep, x).astype(jnp.bfloat16)
        gate_part = mm(x, w_gate[span, :])
        up_part = mm(x, w_up[span, :])
        if c:
            gate_part += total[:, pl.ds(0, hidden_units)]
            up_part += total[:, pl.ds(hidden_units, hidden_units)]
        if c < chunks - 1:
            total[:, pl.ds(0, hidden_units)] = gate_part
            total[:, pl.ds(hidden_units, hidden_units)] = up_part
        else:
            act[0] = (gate_part / (1.0 + jnp.exp(-gate_part)) * up_part).astype(jnp.bfloat16)
    act[1] = mm(perm_dp, act[0]).astype(jnp.bfloat16)
    loads[2].wait()
    for c in range(chunks):
        o1[c] = mm(act[c % 2], w_down[:, pl.ds(c * cols, cols)]).astype(jnp.bfloat16)
        hop(2, c, o1, q1)
    for c in range(chunks):
        wait_all(recv_sems, 2, c, q1)
        q2[c] = mm(perms[1 - c % 2], q1[c]).astype(jnp.bfloat16)
        hop(3, c, q2, q3)
    for c in range(chunks):
        wait_all(recv_sems, 3, c, q3)
        span = pl.ds(c * cols, cols)
        both = mm(weights[c % 2], q3[c])
        out_ref[:, span] = hid[:, span] + (both[:tokens] + both[tokens:])
    for stage, ref in enumerate((s1, s2, o1, q2)):
        for c in range(chunks):
            wait_all(send_sems, stage, c, ref)


def moe(attention, residual, norm_gain, expert_ids, gate_weights, expert_gate, expert_up, expert_down):
    n_dp, n_ep = lax.axis_size("dp"), lax.axis_size("ep")
    tokens, width = residual.shape
    units = expert_gate.shape[2]
    rows = n_dp * n_ep * 2
    chunks = 4
    buf = pltpu.VMEM((chunks, rows, width // chunks), jnp.bfloat16)
    vmem = pl.BlockSpec(memory_space=pltpu.VMEM)
    hbm = pl.BlockSpec(memory_space=pl.ANY)
    return pl.pallas_call(
        functools.partial(moe_kernel, (n_dp, n_ep, chunks)),
        out_shape=jax.ShapeDtypeStruct((tokens, width), jnp.float32),
        in_specs=[vmem] * 5 + [hbm] * 3,
        out_specs=vmem,
        scratch_shapes=[
            pltpu.VMEM((width, units), jnp.bfloat16),
            pltpu.VMEM((width, units), jnp.bfloat16),
            pltpu.VMEM((units, width), jnp.bfloat16),
            pltpu.VMEM((tokens, width), jnp.float32),
            buf,
            buf,
            buf,
            buf,
            pltpu.VMEM((rows, 2 * units), jnp.float32),
            pltpu.VMEM((2, rows, units), jnp.bfloat16),
            buf,
            buf,
            buf,
            buf,
            pltpu.SemaphoreType.DMA((4, chunks)),
            pltpu.SemaphoreType.DMA((4, chunks)),
            pltpu.SemaphoreType.DMA((3,)),
        ],
        compiler_params=pltpu.CompilerParams(
            collective_id=1, has_side_effects=True, vmem_limit_bytes=60 * 2**20
        ),
        name="experts",
    )(
        attention,
        residual,
        norm_gain,
        expert_ids.T,
        gate_weights.T,
        expert_gate,
        expert_up,
        expert_down,
    )


def contract_last(a, b):
    return lax.dot_general(a, b, (((1,), (1,)), ((), ())), preferred_element_type=jnp.float32)


def attend(q, s_old, keys, length, positions, prefix_len, lat):
    s_new = contract_last(q, keys[prefix_len:, :])
    old_pos = lax.broadcasted_iota(jnp.int32, (1, prefix_len), 1)
    s_old = s_old + jnp.where(old_pos < length, 0.0, -1e30)
    new_pos = lax.broadcasted_iota(jnp.int32, s_new.shape, 1)
    s_new = jnp.where(new_pos <= positions, s_new, -1e30)
    top = jnp.maximum(
        jnp.max(s_old, axis=1, keepdims=True), jnp.max(s_new, axis=1, keepdims=True)
    )
    e_old = jnp.exp2((s_old - top) * exp2_scale)
    e_new = jnp.exp2((s_new - top) * exp2_scale)
    weight_sum = jnp.sum(e_old, axis=1, keepdims=True) + jnp.sum(e_new, axis=1, keepdims=True)
    weighted = jnp.dot(
        e_old.astype(jnp.bfloat16), keys[0:prefix_len, 0:lat], preferred_element_type=jnp.float32
    )
    weighted += jnp.dot(
        e_new.astype(jnp.bfloat16), keys[prefix_len:, 0:lat], preferred_element_type=jnp.float32
    )
    return (weighted * (1.0 / weight_sum)).astype(jnp.bfloat16)


SIDE = 4


def attention_kernel(
    lengths_ref,
    sources_ref,
    owner_ref,
    prefix_ref,
    new_ref,
    proj_ref,
    queries_hbm,
    value_up_hbm,
    att_ref,
    decode_ref,
    q_raw,
    value_up,
    q_home,
    q_late,
    scores,
    keys_own,
    late_own,
    late_in,
    late_on,
    rows_own,
    rows_in,
    rows_on,
    news_y,
    news_out,
    news_x,
    proj,
    heads,
    heads_late,
    part,
    part_b,
    pair,
    summed,
    gathered,
    z_recv,
    y_recv,
    dp_recv,
    x_recv,
    pair_recv,
    last_recv,
    sends,
    load_sems,
):
    dp, ep = lax.axis_index("dp"), lax.axis_index("ep")
    x, y = dp // SIDE, lax.rem(dp, SIDE)
    z, core = ep // 2, lax.rem(ep, 2)
    n_dp = SIDE * SIDE
    n_ep = 2 * SIDE
    prefix_part, new_part = prefix_ref.shape[2], new_ref.shape[1]
    prefix_len = prefix_part * n_ep
    shard_rows = prefix_part + new_part
    head_count, lat, vh = value_up.shape
    span = q_raw.shape[2]
    late = span // 4
    home = span - late
    tokens = span // n_ep
    strip = tokens // 2
    block = home // 2
    quad = head_count // 2
    col_part = proj_ref.shape[0]
    cols = col_part * SIDE
    piece = head_count * late // n_dp

    def around(a, k):
        return lax.rem(a + k + SIDE, SIDE)

    def device(x2, y2, z2, core2):
        return (x2 * SIDE + y2, z2 * 2 + core2)

    right_z, left_z = device(x, y, around(z, 1), core), device(x, y, around(z, -1), core)
    right_y, left_y = device(x, around(y, 1), z, core), device(x, around(y, -1), z, core)
    sibling = device(x, y, z, 1 - core)

    load_q = pltpu.make_async_copy(queries_hbm, q_raw, load_sems.at[0])
    load_q.start()
    load_v = pltpu.make_async_copy(value_up_hbm, value_up, load_sems.at[1])
    load_v.start()

    barrier = pltpu.get_barrier_semaphore()

    def hello(to):
        pl.semaphore_signal(barrier, inc=1, device_id=to, device_id_type=MESH)

    partners(n_dp, dp, lambda p: hello((p, ep)))
    for kz in range(1, SIDE):
        for kx in range(SIDE):
            hello(device(around(x, kx), y, around(z, kz), core))
    hello(sibling)

    def send(src, dst, to, send_sem, recv_sem):
        pltpu.make_async_remote_copy(
            src_ref=src,
            dst_ref=dst,
            send_sem=send_sem,
            recv_sem=recv_sem,
            device_id=to,
            device_id_type=MESH,
        ).start()

    def wait(sem, ref):
        pltpu.make_async_copy(ref, ref, sem).wait()

    def key_parts(buf, z2, core2, half):
        at = z2 * 2 + core2
        n, m = (prefix_part // 2, new_part // 2) if half is not None else (prefix_part, new_part)
        half = half or 0
        old = pl.multiple_of(at * prefix_part + half * n, n)
        new = pl.multiple_of(prefix_len + at * new_part + half * m, m)
        return [buf.at[pl.ds(old, n)], buf.at[pl.ds(new, m)]]

    eye_a = lax.broadcasted_iota(jnp.int32, (span, span), 0)
    eye_b = lax.broadcasted_iota(jnp.int32, (span, span), 1)
    eye = jnp.where(eye_a == eye_b, 1.0, 0.0).astype(jnp.bfloat16)
    keys_own[block_rows(ep, prefix_part)] = contract_last(eye, prefix_ref[0]).astype(jnp.bfloat16)
    keys_own[pl.ds(pl.multiple_of(prefix_len + ep * new_part, new_part), new_part)] = new_ref[0]
    proj[block_rows(y, col_part)] = proj_ref[...]

    pl.semaphore_wait(barrier, n_dp - 1 + (SIDE - 1) * SIDE + 1)

    def ring_start(refs, right, left, send_sem, recv):
        for half in (0, 1):
            for ref in refs(0, half):
                send(ref, ref, right, send_sem, recv.at[half])
            for ref in refs(0, 1 - half):
                send(ref, ref, left, send_sem, recv.at[2 + 1 - half])

    def ring_forward(refs, right, left, send_sem, recv, half_ref):
        wait(recv.at[0], half_ref)
        for ref in refs(-1, 0):
            send(ref, ref, right, send_sem, recv.at[4])
        wait(recv.at[3], half_ref)
        for ref in refs(1, 1):
            send(ref, ref, left, send_sem, recv.at[5])

    key_half = keys_own.at[pl.ds(0, shard_rows // 2)]
    key_full = keys_own.at[pl.ds(0, shard_rows)]

    def key_refs(k, half):
        return key_parts(keys_own, around(z, k), core, half)

    def share(k, sem):
        for ref in key_refs(k, None):
            send(ref, ref, sibling, sends.at[0], z_recv.at[sem])

    def everywhere(src, dst, send_sem, recv_sem):
        partners(n_dp, dp, lambda p: send(src(p), dst, (p, ep), send_sem, recv_sem))

    ring_start(key_refs, right_z, left_z, sends.at[0], z_recv)
    share(0, 6)

    def over_axis(along_x, src, dst, send_sem, recv_sem):
        for k in (2, 1, 3):
            to = device(around(x, k), y, z, core) if along_x else device(x, around(y, k), z, core)
            send(src(k), dst, to, send_sem, recv_sem)

    def proj_refs(k, half):
        n = col_part // 2
        start = pl.multiple_of(around(y, k) * col_part + half * n, n)
        return [proj.at[pl.ds(start, n)]]

    load_q.wait()
    for h in range(head_count):
        rows = contract_last(eye, q_raw[h]).astype(jnp.bfloat16)
        late_own[pl.ds(h * late, late)] = rows[home:]
        for b in range(2):
            for e in range(home // tokens):
                at = (h % quad) * block + (e % 2) * block // 2 + (e // 2) * strip
                row = e * tokens + b * strip
                q_home[2 * b + h // quad, pl.ds(at, strip)] = rows[row : row + strip]
    all_late = keys_own.at[pl.ds(0, (n_dp - 1) * piece)]
    all_rows = rows_own.at[pl.ds(0, (n_dp - 1) * piece)]
    everywhere(
        lambda p: late_own.at[block_rows(p, piece)], late_in.at[dp], sends.at[1], dp_recv.at[0]
    )
    late_in[dp] = late_own[block_rows(dp, piece)]
    all_news = keys_own.at[pl.ds(0, (SIDE - 1) * new_part)]
    news_y[y] = new_ref[0]
    over_axis(False, lambda k: news_y.at[y], news_y.at[y], sends.at[3], dp_recv.at[1])

    def score(k):
        at = pl.ds(pl.multiple_of(around(z, k) * 2 * prefix_part, 2 * prefix_part), 2 * prefix_part)

        def step(i, carry):
            scores[i, :, at] = contract_last(q_home[i], keys_own[at])
            return carry

        lax.fori_loop(0, 4, step, 0)

    wait(z_recv.at[6], key_full)
    score(0)
    ring_forward(key_refs, right_z, left_z, sends.at[0], z_recv, key_half)
    wait(z_recv.at[1], key_half)
    share(-1, 7)
    wait(z_recv.at[2], key_half)
    share(1, 8)
    wait(dp_recv.at[0], all_late)

    def stage_late(i, carry):
        slot = jnp.int32(0)
        for s in range(n_dp):
            slot = jnp.maximum(slot, jnp.where(sources_ref[s] == i, s, 0))
        late_on[i] = late_in[slot]
        return carry

    lax.fori_loop(0, n_dp, stage_late, 0)
    everywhere(
        lambda p: late_on.at[p], q_late.at[block_rows(dp, piece)], sends.at[2], dp_recv.at[2]
    )
    q_late[block_rows(dp, piece)] = late_on[dp]
    ring_start(proj_refs, right_y, left_y, sends.at[4], y_recv)
    wait(z_recv.at[7], key_full)
    score(-1)
    wait(z_recv.at[8], key_full)
    score(1)
    wait(z_recv.at[4], key_half)
    wait(z_recv.at[5], key_half)
    share(2, 9)
    load_v.wait()
    wait(z_recv.at[9], key_full)
    score(2)

    def given_to(slot):
        given = jnp.int32(0)
        for i in range(n_dp):
            given = jnp.maximum(given, jnp.where(owner_ref[i] == slot, i, 0))
        return given

    def send_heads(i, refs):
        for ref in refs:
            over_axis(True, lambda k: ref, ref, sends.at[6 + i], x_recv.at[i])

    row = lax.broadcasted_iota(jnp.int32, (quad * block, 1), 0)
    within = row
    for j in range(1, quad):
        within -= jnp.where(row >= j * block, block, 0)
    on_core = jnp.where(within >= block // 2, 1, 0)
    within -= on_core * (block // 2)
    home_pos = ((within // strip) * 2 + on_core) * tokens + lax.rem(within, strip)
    half_rows = SIDE * block // 2

    def home_part(b, half):
        positions = home_pos + b * strip
        i = 2 * b + half
        out = attend(
            q_home[i], scores[i], keys_own, lengths_ref[dp], positions, prefix_len, lat
        )
        for j in range(quad):
            h = half * quad + j
            rows = jnp.dot(
                out[j * block : (j + 1) * block], value_up[h], preferred_element_type=jnp.float32
            ).astype(jnp.bfloat16)
            for c in range(2):
                at = pl.multiple_of(c * half_rows + x * (block // 2), block // 2)
                heads[b, pl.ds(at, block // 2), pl.ds(h * vh, vh)] = rows[
                    c * block // 2 : (c + 1) * block // 2
                ]
        refs = []
        for c in range(2):
            at = pl.multiple_of(c * half_rows + x * (block // 2), block // 2)
            refs.append(
                heads.at[b, pl.ds(at, block // 2), pl.ds(half * quad * vh, quad * vh)]
            )
        send_heads(2 * b + half, refs)

    def wait_heads(i):
        wait(x_recv.at[i], heads.at[0, pl.ds(0, (SIDE - 1) * block // 2)])

    def project(i, rows):
        n = rows.shape[0]
        out = contract_last(rows, proj[...])
        part[i, pl.ds(0, n)] = out
        part_b[i, pl.ds(0, n)] = out.astype(jnp.bfloat16)
        other = part_b.at[i, pl.ds(pl.multiple_of((1 - core) * (n // 2), n // 2), n // 2)]
        send(other, pair.at[i, pl.ds(0, n // 2)], sibling, sends.at[11 + i], pair_recv.at[i])

    def pass_on(i, n, to_z, size, offset):
        wait(pair_recv.at[i], pair.at[i, pl.ds(0, n // 2)])
        mine = part[i, pl.ds(pl.multiple_of(core * (n // 2), n // 2), n // 2)]
        both = mine + pair[i, pl.ds(0, n // 2)].astype(jnp.float32)
        summed[i, pl.ds(0, n // 2)] = both.astype(jnp.bfloat16)
        start = (x * SIDE + z) * tokens + offset
        landing = pl.ds(pl.multiple_of(start, size), size)
        for k in (2, 1, 3, 0):
            xk = around(x, k)
            for j, zk in enumerate(to_z):
                at = pl.multiple_of((xk * len(to_z) + j) * size, size)

                def go():
                    send(
                        summed.at[i, pl.ds(at, size)],
                        gathered.at[landing],
                        device(xk, y, zk, core),
                        sends.at[14],
                        last_recv,
                    )

                if k:
                    go()
                else:
                    pl.when(z != zk)(go)

                    @pl.when(z == zk)
                    def _():
                        gathered[landing] = summed[i, pl.ds(at, size)]

    home_part(0, 0)
    wait(dp_recv.at[1], all_news)
    for k in range(SIDE):
        slot = around(x, k) * SIDE + y
        news_out[k] = news_y[lax.rem(given_to(slot), SIDE)]
    over_axis(True, lambda k: news_out.at[k], news_x.at[x], sends.at[15], dp_recv.at[5])
    news_x[x] = news_out[0]
    home_part(0, 1)
    proj_half = proj.at[pl.ds(0, col_part // 2)]
    ring_forward(proj_refs, right_y, left_y, sends.at[4], y_recv, proj_half)
    wait(dp_recv.at[2], all_late)
    late_row = lax.broadcasted_iota(jnp.int32, (head_count * late, 1), 0)
    late_pos = lax.rem(late_row, late) + home
    late_scores = contract_last(q_late[...], keys_own[0:prefix_len, :])
    out = attend(
        q_late[...], late_scores, keys_own, lengths_ref[dp], late_pos, prefix_len, lat
    )
    for h in range(head_count):
        rows_own[pl.ds(h * late, late)] = jnp.dot(
            out[h * late : (h + 1) * late], value_up[h], preferred_element_type=jnp.float32
        ).astype(jnp.bfloat16)
    everywhere(
        lambda p: rows_own.at[block_rows(p, piece)], rows_in.at[dp], sends.at[5], dp_recv.at[3]
    )
    rows_in[dp] = rows_own[block_rows(dp, piece)]
    home_part(1, 0)
    wait(dp_recv.at[3], all_rows)

    def stage_rows(s, carry):
        at = pl.multiple_of((s // SIDE) * piece, piece)
        rows_on[lax.rem(s, SIDE), pl.ds(at, piece)] = rows_in[sources_ref[s]]
        return carry

    lax.fori_loop(0, n_dp, stage_rows, 0)
    quarter = SIDE * piece
    landing = (
        pl.ds(pl.multiple_of(lax.rem(dp, 2) * quarter, quarter), quarter),
        pl.ds(pl.multiple_of((dp // 2) * vh, vh), vh),
    )
    everywhere(
        lambda p: rows_on.at[lax.rem(p, SIDE)],
        heads_late.at[landing],
        sends.at[16],
        dp_recv.at[4],
    )
    heads_late[landing] = rows_on[y]
    all_late_heads = heads_late.at[pl.ds(0, (n_dp - 1) * quarter * vh // heads_late.shape[1])]
    for i in (1, 2, 4, 5):
        wait(y_recv.at[i], proj_half)
    wait_heads(0)
    wait_heads(1)
    project(0, heads[0])
    home_part(1, 1)
    home_z = tuple(range(home // tokens // 2))
    late_z = (SIDE - 1,)
    home_rows, late_rows = SIDE * block, SIDE * late
    pass_on(0, home_rows, home_z, strip, 0)
    wait(dp_recv.at[4], all_late_heads)
    project(2, heads_late[...])
    pass_on(2, late_rows, late_z, tokens, 0)
    wait_heads(2)
    wait_heads(3)
    project(1, heads[1])
    pass_on(1, home_rows, home_z, strip, strip)
    wait(dp_recv.at[5], all_news)
    decode_ref[0] = news_x[given_to(dp) // SIDE]
    wait(last_recv, gathered.at[pl.ds(0, (n_dp - 1) * tokens)])
    for k in range(SIDE):
        total = gathered[pl.ds(k * SIDE * tokens, tokens)].astype(jnp.float32)
        for j in range(1, SIDE):
            total += gathered[pl.ds((k * SIDE + j) * tokens, tokens)].astype(jnp.float32)
        att_ref[:, pl.ds(k * cols, cols)] = total

    wait(sends.at[0], keys_own.at[pl.ds(0, 3 * shard_rows + 4 * shard_rows)])
    wait(sends.at[1], all_late)
    wait(sends.at[2], all_late)
    wait(sends.at[3], all_news)
    wait(sends.at[15], all_news)
    wait(sends.at[4], proj.at[pl.ds(0, 3 * col_part)])
    wait(sends.at[5], all_rows)
    wait(sends.at[16], all_late_heads)
    for i in range(4):
        wait(sends.at[6 + i], heads.at[0, pl.ds(0, (SIDE - 1) * block // 2)])
    for i in range(2):
        wait(sends.at[11 + i], pair.at[i])
    wait(sends.at[13], pair.at[2, pl.ds(0, late_rows // 2)])
    wait(sends.at[14], gathered.at[pl.ds(0, (n_dp - 1) * tokens)])


def attention(queries, prefix_latents, new_latents, lengths, sources, value_up, out_proj, owner):
    span, head_count, key_width = queries.shape
    _, lat, vh = value_up.shape
    n_dp, n_ep = lax.axis_size("dp"), lax.axis_size("ep")
    late = span // 4
    home = span - late
    late_rows = head_count * late
    prefix_part, new_part = prefix_latents.shape[1], new_latents.shape[1]
    key_rows = (prefix_part + new_part) * n_ep
    rows, col_part = out_proj.shape
    cols = col_part * SIDE
    tokens = span // n_ep
    vmem = pl.BlockSpec(memory_space=pltpu.VMEM)
    smem = pl.BlockSpec(memory_space=pltpu.SMEM)
    hbm = pl.BlockSpec(memory_space=pl.ANY)
    bf16, f32 = jnp.bfloat16, jnp.float32
    return pl.pallas_call(
        attention_kernel,
        out_shape=(
            jax.ShapeDtypeStruct((tokens, cols * SIDE), f32),
            jax.ShapeDtypeStruct(new_latents.shape, bf16),
        ),
        in_specs=[smem] * 3 + [vmem] * 3 + [hbm] * 2,
        out_specs=(vmem, vmem),
        scratch_shapes=[
            pltpu.VMEM((head_count, key_width, span), bf16),
            pltpu.VMEM(value_up.shape, bf16),
            pltpu.VMEM((4, head_count // 2 * (home // 2), key_width), bf16),
            pltpu.VMEM((late_rows, key_width), bf16),
            pltpu.VMEM((4, head_count // 2 * (home // 2), prefix_part * n_ep), f32),
            pltpu.VMEM((key_rows, key_width), bf16),
            pltpu.VMEM((late_rows, key_width), bf16),
            pltpu.VMEM((n_dp, late_rows // n_dp, key_width), bf16),
            pltpu.VMEM((n_dp, late_rows // n_dp, key_width), bf16),
            pltpu.VMEM((late_rows, vh), bf16),
            pltpu.VMEM((n_dp, late_rows // n_dp, vh), bf16),
            pltpu.VMEM((SIDE, SIDE * late_rows // n_dp, vh), bf16),
            pltpu.VMEM((SIDE, new_part, key_width), bf16),
            pltpu.VMEM((SIDE, new_part, key_width), bf16),
            pltpu.VMEM((SIDE, new_part, key_width), bf16),
            pltpu.VMEM((cols, rows), bf16),
            pltpu.VMEM((2, SIDE * home // 2, rows), bf16),
            pltpu.VMEM((SIDE * late, rows), bf16),
            pltpu.VMEM((3, SIDE * home // 2, cols), f32),
            pltpu.VMEM((3, SIDE * home // 2, cols), bf16),
            pltpu.VMEM((3, SIDE * home // 4, cols), bf16),
            pltpu.VMEM((3, SIDE * home // 4, cols), bf16),
            pltpu.VMEM((n_dp * tokens, cols), bf16),
            pltpu.SemaphoreType.DMA((10,)),
            pltpu.SemaphoreType.DMA((6,)),
            pltpu.SemaphoreType.DMA((6,)),
            pltpu.SemaphoreType.DMA((5,)),
            pltpu.SemaphoreType.DMA((3,)),
            pltpu.SemaphoreType.DMA,
            pltpu.SemaphoreType.DMA((17,)),
            pltpu.SemaphoreType.DMA((2,)),
        ],
        compiler_params=pltpu.CompilerParams(
            collective_id=2, has_side_effects=True, vmem_limit_bytes=60 * 2**20
        ),
        name="attention",
    )(
        lengths,
        sources,
        owner,
        prefix_latents.transpose(0, 2, 1),
        new_latents,
        out_proj.T,
        queries.transpose(1, 2, 0),
        value_up,
    )


def shards(
    queries,
    prefix_latents,
    new_latents,
    prefix_lengths,
    span_sources,
    value_up,
    out_proj,
    residual,
    norm_gain,
    expert_gate,
    expert_up,
    expert_down,
    expert_ids,
    gate_weights,
    decode_owner,
):
    attention_sum, decode_latents = attention(
        queries,
        prefix_latents,
        new_latents,
        prefix_lengths,
        span_sources,
        value_up,
        out_proj,
        decode_owner,
    )
    layer_out = moe(
        attention_sum,
        residual,
        norm_gain,
        expert_ids,
        gate_weights,
        expert_gate,
        expert_up,
        expert_down,
    ).astype(jnp.bfloat16)
    return (layer_out, decode_latents)


def solution(mesh):
    return jax.shard_map(
        shards,
        mesh=mesh,
        in_specs=(
            P("dp", "ep", None),
            P("dp", "ep", None),
            P("dp", "ep", None),
            P(),
            P(),
            P("ep", None, None),
            P("ep", "dp"),
            P(("dp", "ep"), None),
            P(),
            P(("dp", "ep"), None, None),
            P(("dp", "ep"), None, None),
            P(("dp", "ep"), None, None),
            P(("dp", "ep"), None),
            P(("dp", "ep"), None),
            P(),
        ),
        out_specs=(P(("dp", "ep"), None), P("dp", "ep", None)),
        check_vma=False,
    )
```

```python
import functools
import math

import jax
import jax.numpy as jnp
from jax import lax
from jax.experimental import pallas as pl
from jax.experimental.pallas import tpu as pltpu
from jax.sharding import PartitionSpec as P

TOP = 8


score_scale = 192.0 ** (-0.5)
exp2_scale = score_scale * math.log2(math.e)
norm_eps = 1e-06


MESH = pl.DeviceIdType.MESH


def partners(count, me, each):
    def step(k, carry):
        each(lax.rem(me + k, count))
        return carry

    lax.fori_loop(1, count, step, 0)


def block_rows(start, size):
    return pl.ds(pl.multiple_of(start * size, size), size)


def moe_kernel(
    sizes,
    att_ref,
    res_ref,
    gain_ref,
    ids_ref,
    gates_ref,
    gate_hbm,
    up_hbm,
    down_hbm,
    out_ref,
    w_gate,
    w_up,
    w_down,
    hid,
    s1,
    r1,
    s2,
    r2,
    total,
    act,
    o1,
    q1,
    q2,
    q3,
    send_sems,
    recv_sems,
    weight_sems,
):
    n_dp, n_ep, chunks = sizes
    dp, ep = lax.axis_index("dp"), lax.axis_index("ep")
    rows = n_dp * n_ep * 2
    dp_block, ep_block = 2 * n_ep, 2 * n_dp
    cols = hid.shape[1] // chunks
    tokens = hid.shape[0]
    hidden_units = w_gate.shape[1]

    loads = [
        pltpu.make_async_copy(src.at[0], dst, weight_sems.at[i])
        for i, (src, dst) in enumerate(((gate_hbm, w_gate), (up_hbm, w_up), (down_hbm, w_down)))
    ]
    barrier = pltpu.get_barrier_semaphore()
    partners(
        n_dp,
        dp,
        lambda p: pl.semaphore_signal(barrier, inc=1, device_id=(p, ep), device_id_type=MESH),
    )
    partners(
        n_ep,
        ep,
        lambda p: pl.semaphore_signal(barrier, inc=1, device_id=(dp, p), device_id_type=MESH),
    )

    def send_dp(stage, c, src, dst):
        def each(p):
            pltpu.make_async_remote_copy(
                src_ref=src.at[c, block_rows(p, dp_block)],
                dst_ref=dst.at[c, block_rows(dp, dp_block)],
                send_sem=send_sems.at[stage, c],
                recv_sem=recv_sems.at[stage, c],
                device_id=(p, ep),
                device_id_type=MESH,
            ).start()

        partners(n_dp, dp, each)
        dst[c, block_rows(dp, dp_block)] = src[c, block_rows(dp, dp_block)]


    def send_ep(stage, c, src, dst):
        def each(p):
            pltpu.make_async_remote_copy(
                src_ref=src.at[c, block_rows(p, ep_block)],
                dst_ref=dst.at[c, block_rows(ep, ep_block)],
                send_sem=send_sems.at[stage, c],
                recv_sem=recv_sems.at[stage, c],
                device_id=(dp, p),
                device_id_type=MESH,
            ).start()

        partners(n_ep, ep, each)
        dst[c, block_rows(ep, ep_block)] = src[c, block_rows(ep, ep_block)]

    def over_dp(stage, c):
        return (c % 2 == 0) == (stage in (0, 3))

    def hop(stage, c, src, dst):
        (send_dp if over_dp(stage, c) else send_ep)(stage, c, src, dst)

    def wait_all(sems, stage, c, ref):
        size = rows - (dp_block if over_dp(stage, c) else ep_block)
        part = ref.at[c, pl.ds(0, size)]
        pltpu.make_async_copy(part, part, sems.at[stage, c]).wait()

    def mm(a, b):
        return jnp.dot(a, b, preferred_element_type=jnp.float32)

    slot = lax.broadcasted_iota(jnp.int32, (rows, tokens), 0)
    named = jnp.zeros((rows, tokens), jnp.float32)
    weight = jnp.zeros((rows, tokens), jnp.float32)
    for k in range(TOP):
        hit = ids_ref[k : k + 1, :] == (slot >> 1)
        named += jnp.where(hit, 1.0, 0.0)
        weight += jnp.where(hit, gates_ref[k : k + 1, :], 0.0)
    first = lax.broadcasted_iota(jnp.int32, (tokens, tokens), 0)
    second = lax.broadcasted_iota(jnp.int32, (tokens, tokens), 1)
    before = jnp.where(first < second, 1.0, 0.0).astype(jnp.bfloat16)
    same = jnp.where(first == second, 1.0, 0.0).astype(jnp.bfloat16)
    chosen = mm(named.astype(jnp.bfloat16), before) == (slot & 1).astype(jnp.float32)
    pick = jnp.where(chosen, named, 0.0).astype(jnp.bfloat16)
    weight = jnp.where(chosen, weight, 0.0)
    weight_high = weight.astype(jnp.bfloat16)
    weight_low = (weight - weight_high.astype(jnp.float32)).astype(jnp.bfloat16)
    weight_high = contract_last(same, weight_high).astype(jnp.bfloat16)
    weight_low = contract_last(same, weight_low).astype(jnp.bfloat16)
    weights = jnp.concatenate([weight_high, weight_low], axis=0)
    to = lax.broadcasted_iota(jnp.int32, (rows, rows), 0)
    frm = lax.broadcasted_iota(jnp.int32, (rows, rows), 1)
    by_ep = lax.rem(to >> 1, n_dp) * dp_block + (to // ep_block) * 2 + (to & 1)
    by_dp = lax.rem(to >> 1, n_ep) * ep_block + (to // dp_block) * 2 + (to & 1)
    perm_ep = jnp.where(frm == by_ep, 1.0, 0.0).astype(jnp.bfloat16)
    perm_dp = jnp.where(frm == by_dp, 1.0, 0.0).astype(jnp.bfloat16)
    picks = (pick, mm(perm_ep, pick).astype(jnp.bfloat16))
    weights = (weights, contract_last(weights, perm_ep).astype(jnp.bfloat16))
    perms = (perm_ep, perm_dp)

    hidden = res_ref[...].astype(jnp.float32) + att_ref[...].astype(jnp.float32)
    hid[...] = hidden
    mean_square = jnp.mean(hidden * hidden, axis=1, keepdims=True)
    scale = lax.rsqrt(mean_square + norm_eps)

    pl.semaphore_wait(barrier, n_dp + n_ep - 2)

    for c in range(chunks):
        span = pl.ds(c * cols, cols)
        normed = (hid[:, span] * scale * gain_ref[span].astype(jnp.float32).reshape(1, cols)).astype(
            jnp.bfloat16
        )
        s1[c] = mm(picks[c % 2], normed).astype(jnp.bfloat16)
        hop(0, c, s1, r1)
    loads[0].start()
    loads[1].start()
    for c in range(chunks):
        wait_all(recv_sems, 0, c, r1)
        s2[c] = mm(perms[c % 2], r1[c]).astype(jnp.bfloat16)
        hop(1, c, s2, r2)
    loads[2].start()
    loads[0].wait()
    loads[1].wait()
    for c in range(chunks):
        wait_all(recv_sems, 1, c, r2)
        span = pl.ds(c * cols, cols)
        x = r2[c]
        if c % 2:
            x = mm(perm_ep, x).astype(jnp.bfloat16)
        gate_part = mm(x, w_gate[span, :])
        up_part = mm(x, w_up[span, :])
        if c:
            gate_part += total[:, pl.ds(0, hidden_units)]
            up_part += total[:, pl.ds(hidden_units, hidden_units)]
        if c < chunks - 1:
            total[:, pl.ds(0, hidden_units)] = gate_part
            total[:, pl.ds(hidden_units, hidden_units)] = up_part
        else:
            act[0] = (gate_part / (1.0 + jnp.exp(-gate_part)) * up_part).astype(jnp.bfloat16)
    act[1] = mm(perm_dp, act[0]).astype(jnp.bfloat16)
    loads[2].wait()
    for c in range(chunks):
        o1[c] = mm(act[c % 2], w_down[:, pl.ds(c * cols, cols)]).astype(jnp.bfloat16)
        hop(2, c, o1, q1)
    for c in range(chunks):
        wait_all(recv_sems, 2, c, q1)
        q2[c] = mm(perms[1 - c % 2], q1[c]).astype(jnp.bfloat16)
        hop(3, c, q2, q3)
    for c in range(chunks):
        wait_all(recv_sems, 3, c, q3)
        span = pl.ds(c * cols, cols)
        both = mm(weights[c % 2], q3[c])
        out_ref[:, span] = hid[:, span] + (both[:tokens] + both[tokens:])
    for stage, ref in enumerate((s1, s2, o1, q2)):
        for c in range(chunks):
            wait_all(send_sems, stage, c, ref)


def moe(attention, residual, norm_gain, expert_ids, gate_weights, expert_gate, expert_up, expert_down):
    n_dp, n_ep = lax.axis_size("dp"), lax.axis_size("ep")
    tokens, width = residual.shape
    units = expert_gate.shape[2]
    rows = n_dp * n_ep * 2
    chunks = 4
    buf = pltpu.VMEM((chunks, rows, width // chunks), jnp.bfloat16)
    vmem = pl.BlockSpec(memory_space=pltpu.VMEM)
    hbm = pl.BlockSpec(memory_space=pl.ANY)
    return pl.pallas_call(
        functools.partial(moe_kernel, (n_dp, n_ep, chunks)),
        out_shape=jax.ShapeDtypeStruct((tokens, width), jnp.float32),
        in_specs=[vmem] * 5 + [hbm] * 3,
        out_specs=vmem,
        scratch_shapes=[
            pltpu.VMEM((width, units), jnp.bfloat16),
            pltpu.VMEM((width, units), jnp.bfloat16),
            pltpu.VMEM((units, width), jnp.bfloat16),
            pltpu.VMEM((tokens, width), jnp.float32),
            buf,
            buf,
            buf,
            buf,
            pltpu.VMEM((rows, 2 * units), jnp.float32),
            pltpu.VMEM((2, rows, units), jnp.bfloat16),
            buf,
            buf,
            buf,
            buf,
            pltpu.SemaphoreType.DMA((4, chunks)),
            pltpu.SemaphoreType.DMA((4, chunks)),
            pltpu.SemaphoreType.DMA((3,)),
        ],
        compiler_params=pltpu.CompilerParams(
            collective_id=1, has_side_effects=True, vmem_limit_bytes=60 * 2**20
        ),
        name="experts",
    )(
        attention,
        residual,
        norm_gain,
        expert_ids.T,
        gate_weights.T,
        expert_gate,
        expert_up,
        expert_down,
    )


def contract_last(a, b):
    return lax.dot_general(a, b, (((1,), (1,)), ((), ())), preferred_element_type=jnp.float32)


def attend(q, s_old, keys, length, positions, prefix_len, lat):
    s_new = contract_last(q, keys[prefix_len:, :])
    old_pos = lax.broadcasted_iota(jnp.int32, (1, prefix_len), 1)
    s_old = s_old + jnp.where(old_pos < length, 0.0, -1e30)
    new_pos = lax.broadcasted_iota(jnp.int32, s_new.shape, 1)
    s_new = jnp.where(new_pos <= positions, s_new, -1e30)
    top = jnp.maximum(
        jnp.max(s_old, axis=1, keepdims=True), jnp.max(s_new, axis=1, keepdims=True)
    )
    e_old = jnp.exp2((s_old - top) * exp2_scale)
    e_new = jnp.exp2((s_new - top) * exp2_scale)
    weight_sum = jnp.sum(e_old, axis=1, keepdims=True) + jnp.sum(e_new, axis=1, keepdims=True)
    weighted = jnp.dot(
        e_old.astype(jnp.bfloat16), keys[0:prefix_len, 0:lat], preferred_element_type=jnp.float32
    )
    weighted += jnp.dot(
        e_new.astype(jnp.bfloat16), keys[prefix_len:, 0:lat], preferred_element_type=jnp.float32
    )
    return (weighted * (1.0 / weight_sum)).astype(jnp.bfloat16)


SIDE = 4


def attention_kernel(
    lengths_ref,
    sources_ref,
    owner_ref,
    prefix_ref,
    new_ref,
    proj_ref,
    queries_hbm,
    value_up_hbm,
    att_ref,
    decode_ref,
    q_raw,
    value_up,
    q_home,
    q_late,
    scores,
    keys_own,
    late_own,
    late_in,
    late_on,
    rows_own,
    rows_in,
    rows_on,
    news_y,
    news_out,
    news_x,
    proj,
    heads,
    heads_late,
    part,
    part_b,
    pair,
    summed,
    gathered,
    z_recv,
    y_recv,
    dp_recv,
    x_recv,
    pair_recv,
    last_recv,
    sends,
    load_sems,
):
    dp, ep = lax.axis_index("dp"), lax.axis_index("ep")
    x, y = dp // SIDE, lax.rem(dp, SIDE)
    z, core = ep // 2, lax.rem(ep, 2)
    n_dp = SIDE * SIDE
    n_ep = 2 * SIDE
    prefix_part, new_part = prefix_ref.shape[2], new_ref.shape[1]
    prefix_len = prefix_part * n_ep
    shard_rows = prefix_part + new_part
    head_count, lat, vh = value_up.shape
    span = q_raw.shape[2]
    late = span // 4
    home = span - late
    tokens = span // n_ep
    strip = tokens // 2
    block = home // 2
    quad = head_count // 2
    col_part = proj_ref.shape[0]
    cols = col_part * SIDE
    piece = head_count * late // n_dp

    def around(a, k):
        return lax.rem(a + k + SIDE, SIDE)

    def device(x2, y2, z2, core2):
        return (x2 * SIDE + y2, z2 * 2 + core2)

    right_z, left_z = device(x, y, around(z, 1), core), device(x, y, around(z, -1), core)
    right_y, left_y = device(x, around(y, 1), z, core), device(x, around(y, -1), z, core)
    sibling = device(x, y, z, 1 - core)

    load_q = pltpu.make_async_copy(queries_hbm, q_raw, load_sems.at[0])
    load_q.start()
    load_v = pltpu.make_async_copy(value_up_hbm, value_up, load_sems.at[1])
    load_v.start()

    barrier = pltpu.get_barrier_semaphore()

    def hello(to):
        pl.semaphore_signal(barrier, inc=1, device_id=to, device_id_type=MESH)

    partners(n_dp, dp, lambda p: hello((p, ep)))
    for kz in range(1, SIDE):
        for kx in range(SIDE):
            hello(device(around(x, kx), y, around(z, kz), core))
    hello(sibling)

    def send(src, dst, to, send_sem, recv_sem):
        pltpu.make_async_remote_copy(
            src_ref=src,
            dst_ref=dst,
            send_sem=send_sem,
            recv_sem=recv_sem,
            device_id=to,
            device_id_type=MESH,
        ).start()

    def wait(sem, ref):
        pltpu.make_async_copy(ref, ref, sem).wait()

    def key_parts(buf, z2, core2, half):
        at = z2 * 2 + core2
        n, m = (prefix_part // 2, new_part // 2) if half is not None else (prefix_part, new_part)
        half = half or 0
        old = pl.multiple_of(at * prefix_part + half * n, n)
        new = pl.multiple_of(prefix_len + at * new_part + half * m, m)
        return [buf.at[pl.ds(old, n)], buf.at[pl.ds(new, m)]]

    eye_a = lax.broadcasted_iota(jnp.int32, (span, span), 0)
    eye_b = lax.broadcasted_iota(jnp.int32, (span, span), 1)
    eye = jnp.where(eye_a == eye_b, 1.0, 0.0).astype(jnp.bfloat16)
    keys_own[block_rows(ep, prefix_part)] = contract_last(eye, prefix_ref[0]).astype(jnp.bfloat16)
    keys_own[pl.ds(pl.multiple_of(prefix_len + ep * new_part, new_part), new_part)] = new_ref[0]
    proj[block_rows(y, col_part)] = proj_ref[...]

    pl.semaphore_wait(barrier, n_dp - 1 + (SIDE - 1) * SIDE + 1)

    def ring_start(refs, right, left, send_sem, recv):
        for half in (0, 1):
            for ref in refs(0, half):
                send(ref, ref, right, send_sem, recv.at[half])
            for ref in refs(0, 1 - half):
                send(ref, ref, left, send_sem, recv.at[2 + 1 - half])

    def ring_forward(refs, right, left, send_sem, recv, half_ref):
        wait(recv.at[0], half_ref)
        for ref in refs(-1, 0):
            send(ref, ref, right, send_sem, recv.at[4])
        wait(recv.at[3], half_ref)
        for ref in refs(1, 1):
            send(ref, ref, left, send_sem, recv.at[5])

    key_half = keys_own.at[pl.ds(0, shard_rows // 2)]
    key_full = keys_own.at[pl.ds(0, shard_rows)]

    def key_refs(k, half):
        return key_parts(keys_own, around(z, k), core, half)

    def share(k, sem):
        for ref in key_refs(k, None):
            send(ref, ref, sibling, sends.at[0], z_recv.at[sem])

    def everywhere(src, dst, send_sem, recv_sem):
        partners(n_dp, dp, lambda p: send(src(p), dst, (p, ep), send_sem, recv_sem))

    ring_start(key_refs, right_z, left_z, sends.at[0], z_recv)
    share(0, 6)

    def over_axis(along_x, src, dst, send_sem, recv_sem):
        for k in (2, 1, 3):
            to = device(around(x, k), y, z, core) if along_x else device(x, around(y, k), z, core)
            send(src(k), dst, to, send_sem, recv_sem)

    def proj_refs(k, half):
        n = col_part // 2
        start = pl.multiple_of(around(y, k) * col_part + half * n, n)
        return [proj.at[pl.ds(start, n)]]

    load_q.wait()
    for h in range(head_count):
        rows = contract_last(eye, q_raw[h]).astype(jnp.bfloat16)
        late_own[pl.ds(h * late, late)] = rows[home:]
        for b in range(2):
            for e in range(home // tokens):
                at = (h % quad) * block + (e % 2) * block // 2 + (e // 2) * strip
                row = e * tokens + b * strip
                q_home[2 * b + h // quad, pl.ds(at, strip)] = rows[row : row + strip]
    all_late = keys_own.at[pl.ds(0, (n_dp - 1) * piece)]
    all_rows = rows_own.at[pl.ds(0, (n_dp - 1) * piece)]
    everywhere(
        lambda p: late_own.at[block_rows(p, piece)], late_in.at[dp], sends.at[1], dp_recv.at[0]
    )
    late_in[dp] = late_own[block_rows(dp, piece)]
    all_news = keys_own.at[pl.ds(0, (SIDE - 1) * new_part)]
    news_y[y] = new_ref[0]
    over_axis(False, lambda k: news_y.at[y], news_y.at[y], sends.at[3], dp_recv.at[1])

    def score(k):
        at = pl.ds(pl.multiple_of(around(z, k) * 2 * prefix_part, 2 * prefix_part), 2 * prefix_part)

        def step(i, carry):
            scores[i, :, at] = contract_last(q_home[i], keys_own[at])
            return carry

        lax.fori_loop(0, 4, step, 0)

    wait(z_recv.at[6], key_full)
    score(0)
    ring_forward(key_refs, right_z, left_z, sends.at[0], z_recv, key_half)
    wait(z_recv.at[1], key_half)
    share(-1, 7)
    wait(z_recv.at[2], key_half)
    share(1, 8)
    wait(dp_recv.at[0], all_late)

    def stage_late(i, carry):
        slot = jnp.int32(0)
        for s in range(n_dp):
            slot = jnp.maximum(slot, jnp.where(sources_ref[s] == i, s, 0))
        late_on[i] = late_in[slot]
        return carry

    lax.fori_loop(0, n_dp, stage_late, 0)
    everywhere(
        lambda p: late_on.at[p], q_late.at[block_rows(dp, piece)], sends.at[2], dp_recv.at[2]
    )
    q_late[block_rows(dp, piece)] = late_on[dp]
    ring_start(proj_refs, right_y, left_y, sends.at[4], y_recv)
    wait(z_recv.at[7], key_full)
    score(-1)
    wait(z_recv.at[8], key_full)
    score(1)
    wait(z_recv.at[4], key_half)
    wait(z_recv.at[5], key_half)
    share(2, 9)
    load_v.wait()
    wait(z_recv.at[9], key_full)
    score(2)

    def given_to(slot):
        given = jnp.int32(0)
        for i in range(n_dp):
            given = jnp.maximum(given, jnp.where(owner_ref[i] == slot, i, 0))
        return given

    def send_heads(i, refs):
        for ref in refs:
            over_axis(True, lambda k: ref, ref, sends.at[6 + i], x_recv.at[i])

    row = lax.broadcasted_iota(jnp.int32, (quad * block, 1), 0)
    within = row
    for j in range(1, quad):
        within -= jnp.where(row >= j * block, block, 0)
    on_core = jnp.where(within >= block // 2, 1, 0)
    within -= on_core * (block // 2)
    home_pos = ((within // strip) * 2 + on_core) * tokens + lax.rem(within, strip)
    half_rows = SIDE * block // 2

    def home_part(b, half):
        positions = home_pos + b * strip
        i = 2 * b + half
        out = attend(
            q_home[i], scores[i], keys_own, lengths_ref[dp], positions, prefix_len, lat
        )
        for j in range(quad):
            h = half * quad + j
            rows = jnp.dot(
                out[j * block : (j + 1) * block], value_up[h], preferred_element_type=jnp.float32
            ).astype(jnp.bfloat16)
            for c in range(2):
                at = pl.multiple_of(c * half_rows + x * (block // 2), block // 2)
                heads[b, pl.ds(at, block // 2), pl.ds(h * vh, vh)] = rows[
                    c * block // 2 : (c + 1) * block // 2
                ]
        refs = []
        for c in range(2):
            at = pl.multiple_of(c * half_rows + x * (block // 2), block // 2)
            refs.append(
                heads.at[b, pl.ds(at, block // 2), pl.ds(half * quad * vh, quad * vh)]
            )
        send_heads(2 * b + half, refs)

    def wait_heads(i):
        wait(x_recv.at[i], heads.at[0, pl.ds(0, (SIDE - 1) * block // 2)])

    def project(i, rows):
        n = rows.shape[0]
        out = contract_last(rows, proj[...])
        part[i, pl.ds(0, n)] = out
        part_b[i, pl.ds(0, n)] = out.astype(jnp.bfloat16)
        other = part_b.at[i, pl.ds(pl.multiple_of((1 - core) * (n // 2), n // 2), n // 2)]
        send(other, pair.at[i, pl.ds(0, n // 2)], sibling, sends.at[11 + i], pair_recv.at[i])

    def pass_on(i, n, to_z, size, offset):
        wait(pair_recv.at[i], pair.at[i, pl.ds(0, n // 2)])
        mine = part[i, pl.ds(pl.multiple_of(core * (n // 2), n // 2), n // 2)]
        both = mine + pair[i, pl.ds(0, n // 2)].astype(jnp.float32)
        summed[i, pl.ds(0, n // 2)] = both.astype(jnp.bfloat16)
        start = (x * SIDE + z) * tokens + offset
        landing = pl.ds(pl.multiple_of(start, size), size)
        for k in (2, 1, 3, 0):
            xk = around(x, k)
            for j, zk in enumerate(to_z):
                at = pl.multiple_of((xk * len(to_z) + j) * size, size)

                def go():
                    send(
                        summed.at[i, pl.ds(at, size)],
                        gathered.at[landing],
                        device(xk, y, zk, core),
                        sends.at[14],
                        last_recv,
                    )

                if k:
                    go()
                else:
                    pl.when(z != zk)(go)

                    @pl.when(z == zk)
                    def _():
                        gathered[landing] = summed[i, pl.ds(at, size)]

    home_part(0, 0)
    wait(dp_recv.at[1], all_news)
    for k in range(SIDE):
        slot = around(x, k) * SIDE + y
        news_out[k] = news_y[lax.rem(given_to(slot), SIDE)]
    over_axis(True, lambda k: news_out.at[k], news_x.at[x], sends.at[15], dp_recv.at[5])
    news_x[x] = news_out[0]
    home_part(0, 1)
    proj_half = proj.at[pl.ds(0, col_part // 2)]
    ring_forward(proj_refs, right_y, left_y, sends.at[4], y_recv, proj_half)
    wait(dp_recv.at[2], all_late)
    late_row = lax.broadcasted_iota(jnp.int32, (head_count * late, 1), 0)
    late_pos = lax.rem(late_row, late) + home
    late_scores = contract_last(q_late[...], keys_own[0:prefix_len, :])
    out = attend(
        q_late[...], late_scores, keys_own, lengths_ref[dp], late_pos, prefix_len, lat
    )
    for h in range(head_count):
        rows_own[pl.ds(h * late, late)] = jnp.dot(
            out[h * late : (h + 1) * late], value_up[h], preferred_element_type=jnp.float32
        ).astype(jnp.bfloat16)
    everywhere(
        lambda p: rows_own.at[block_rows(p, piece)], rows_in.at[dp], sends.at[5], dp_recv.at[3]
    )
    rows_in[dp] = rows_own[block_rows(dp, piece)]
    home_part(1, 0)
    wait(dp_recv.at[3], all_rows)

    def stage_rows(s, carry):
        at = pl.multiple_of((s // SIDE) * piece, piece)
        rows_on[lax.rem(s, SIDE), pl.ds(at, piece)] = rows_in[sources_ref[s]]
        return carry

    lax.fori_loop(0, n_dp, stage_rows, 0)
    quarter = SIDE * piece
    landing = (
        pl.ds(pl.multiple_of(lax.rem(dp, 2) * quarter, quarter), quarter),
        pl.ds(pl.multiple_of((dp // 2) * vh, vh), vh),
    )
    everywhere(
        lambda p: rows_on.at[lax.rem(p, SIDE)],
        heads_late.at[landing],
        sends.at[16],
        dp_recv.at[4],
    )
    heads_late[landing] = rows_on[y]
    all_late_heads = heads_late.at[pl.ds(0, (n_dp - 1) * quarter * vh // heads_late.shape[1])]
    for i in (1, 2, 4, 5):
        wait(y_recv.at[i], proj_half)
    wait_heads(0)
    wait_heads(1)
    project(0, heads[0])
    home_part(1, 1)
    home_z = tuple(range(home // tokens // 2))
    late_z = (SIDE - 1,)
    home_rows, late_rows = SIDE * block, SIDE * late
    pass_on(0, home_rows, home_z, strip, 0)
    wait(dp_recv.at[4], all_late_heads)
    project(2, heads_late[...])
    pass_on(2, late_rows, late_z, tokens, 0)
    wait_heads(2)
    wait_heads(3)
    project(1, heads[1])
    pass_on(1, home_rows, home_z, strip, strip)
    wait(dp_recv.at[5], all_news)
    decode_ref[0] = news_x[given_to(dp) // SIDE]
    wait(last_recv, gathered.at[pl.ds(0, (n_dp - 1) * tokens)])
    for k in range(SIDE):
        total = gathered[pl.ds(k * SIDE * tokens, tokens)].astype(jnp.float32)
        for j in range(1, SIDE):
            total += gathered[pl.ds((k * SIDE + j) * tokens, tokens)].astype(jnp.float32)
        att_ref[:, pl.ds(k * cols, cols)] = total

    wait(sends.at[0], keys_own.at[pl.ds(0, 3 * shard_rows + 4 * shard_rows)])
    wait(sends.at[1], all_late)
    wait(sends.at[2], all_late)
    wait(sends.at[3], all_news)
    wait(sends.at[15], all_news)
    wait(sends.at[4], proj.at[pl.ds(0, 3 * col_part)])
    wait(sends.at[5], all_rows)
    wait(sends.at[16], all_late_heads)
    for i in range(4):
        wait(sends.at[6 + i], heads.at[0, pl.ds(0, (SIDE - 1) * block // 2)])
    for i in range(2):
        wait(sends.at[11 + i], pair.at[i])
    wait(sends.at[13], pair.at[2, pl.ds(0, late_rows // 2)])
    wait(sends.at[14], gathered.at[pl.ds(0, (n_dp - 1) * tokens)])


def attention(queries, prefix_latents, new_latents, lengths, sources, value_up, out_proj, owner):
    span, head_count, key_width = queries.shape
    _, lat, vh = value_up.shape
    n_dp, n_ep = lax.axis_size("dp"), lax.axis_size("ep")
    late = span // 4
    home = span - late
    late_rows = head_count * late
    prefix_part, new_part = prefix_latents.shape[1], new_latents.shape[1]
    key_rows = (prefix_part + new_part) * n_ep
    rows, col_part = out_proj.shape
    cols = col_part * SIDE
    tokens = span // n_ep
    vmem = pl.BlockSpec(memory_space=pltpu.VMEM)
    smem = pl.BlockSpec(memory_space=pltpu.SMEM)
    hbm = pl.BlockSpec(memory_space=pl.ANY)
    bf16, f32 = jnp.bfloat16, jnp.float32
    return pl.pallas_call(
        attention_kernel,
        out_shape=(
            jax.ShapeDtypeStruct((tokens, cols * SIDE), f32),
            jax.ShapeDtypeStruct(new_latents.shape, bf16),
        ),
        in_specs=[smem] * 3 + [vmem] * 3 + [hbm] * 2,
        out_specs=(vmem, vmem),
        scratch_shapes=[
            pltpu.VMEM((head_count, key_width, span), bf16),
            pltpu.VMEM(value_up.shape, bf16),
            pltpu.VMEM((4, head_count // 2 * (home // 2), key_width), bf16),
            pltpu.VMEM((late_rows, key_width), bf16),
            pltpu.VMEM((4, head_count // 2 * (home // 2), prefix_part * n_ep), f32),
            pltpu.VMEM((key_rows, key_width), bf16),
            pltpu.VMEM((late_rows, key_width), bf16),
            pltpu.VMEM((n_dp, late_rows // n_dp, key_width), bf16),
            pltpu.VMEM((n_dp, late_rows // n_dp, key_width), bf16),
            pltpu.VMEM((late_rows, vh), bf16),
            pltpu.VMEM((n_dp, late_rows // n_dp, vh), bf16),
            pltpu.VMEM((SIDE, SIDE * late_rows // n_dp, vh), bf16),
            pltpu.VMEM((SIDE, new_part, key_width), bf16),
            pltpu.VMEM((SIDE, new_part, key_width), bf16),
            pltpu.VMEM((SIDE, new_part, key_width), bf16),
            pltpu.VMEM((cols, rows), bf16),
            pltpu.VMEM((2, SIDE * home // 2, rows), bf16),
            pltpu.VMEM((SIDE * late, rows), bf16),
            pltpu.VMEM((3, SIDE * home // 2, cols), f32),
            pltpu.VMEM((3, SIDE * home // 2, cols), bf16),
            pltpu.VMEM((3, SIDE * home // 4, cols), bf16),
            pltpu.VMEM((3, SIDE * home // 4, cols), bf16),
            pltpu.VMEM((n_dp * tokens, cols), bf16),
            pltpu.SemaphoreType.DMA((10,)),
            pltpu.SemaphoreType.DMA((6,)),
            pltpu.SemaphoreType.DMA((6,)),
            pltpu.SemaphoreType.DMA((5,)),
            pltpu.SemaphoreType.DMA((3,)),
            pltpu.SemaphoreType.DMA,
            pltpu.SemaphoreType.DMA((17,)),
            pltpu.SemaphoreType.DMA((2,)),
        ],
        compiler_params=pltpu.CompilerParams(
            collective_id=2, has_side_effects=True, vmem_limit_bytes=60 * 2**20
        ),
        name="attention",
    )(
        lengths,
        sources,
        owner,
        prefix_latents.transpose(0, 2, 1),
        new_latents,
        out_proj.T,
        queries.transpose(1, 2, 0),
        value_up,
    )


def shards(
    queries,
    prefix_latents,
    new_latents,
    prefix_lengths,
    span_sources,
    value_up,
    out_proj,
    residual,
    norm_gain,
    expert_gate,
    expert_up,
    expert_down,
    expert_ids,
    gate_weights,
    decode_owner,
):
    attention_sum, decode_latents = attention(
        queries,
        prefix_latents,
        new_latents,
        prefix_lengths,
        span_sources,
        value_up,
        out_proj,
        decode_owner,
    )
    layer_out = moe(
        attention_sum,
        residual,
        norm_gain,
        expert_ids,
        gate_weights,
        expert_gate,
        expert_up,
        expert_down,
    ).astype(jnp.bfloat16)
    return (layer_out, decode_latents)


def solution(mesh):
    return jax.shard_map(
        shards,
        mesh=mesh,
        in_specs=(
            P("dp", "ep", None),
            P("dp", "ep", None),
            P("dp", "ep", None),
            P(),
            P(),
            P("ep", None, None),
            P("ep", "dp"),
            P(("dp", "ep"), None),
            P(),
            P(("dp", "ep"), None, None),
            P(("dp", "ep"), None, None),
            P(("dp", "ep"), None, None),
            P(("dp", "ep"), None),
            P(("dp", "ep"), None),
            P(),
        ),
        out_specs=(P(("dp", "ep"), None), P("dp", "ep", None)),
        check_vma=False,
    )
```

```python
import functools
import math

import jax
import jax.numpy as jnp
from jax import lax
from jax.experimental import pallas as pl
from jax.experimental.pallas import tpu as pltpu
from jax.sharding import PartitionSpec as P

TOP = 8


score_scale = 192.0 ** (-0.5)
exp2_scale = score_scale * math.log2(math.e)
norm_eps = 1e-06


MESH = pl.DeviceIdType.MESH


def partners(count, me, each):
    def step(k, carry):
        each(lax.rem(me + k, count))
        return carry

    lax.fori_loop(1, count, step, 0)


def block_rows(start, size):
    return pl.ds(pl.multiple_of(start * size, size), size)


def moe_kernel(
    sizes,
    att_ref,
    res_ref,
    gain_ref,
    ids_ref,
    gates_ref,
    gate_hbm,
    up_hbm,
    down_hbm,
    out_ref,
    w_gate,
    w_up,
    w_down,
    hid,
    s1,
    r1,
    s2,
    r2,
    total,
    act,
    o1,
    q1,
    q2,
    q3,
    send_sems,
    recv_sems,
    weight_sems,
):
    n_dp, n_ep, chunks = sizes
    dp, ep = lax.axis_index("dp"), lax.axis_index("ep")
    rows = n_dp * n_ep * 2
    dp_block, ep_block = 2 * n_ep, 2 * n_dp
    cols = hid.shape[1] // chunks
    tokens = hid.shape[0]
    hidden_units = w_gate.shape[1]

    loads = [
        pltpu.make_async_copy(src.at[0], dst, weight_sems.at[i])
        for i, (src, dst) in enumerate(((gate_hbm, w_gate), (up_hbm, w_up), (down_hbm, w_down)))
    ]
    for load in loads:
        load.start()

    barrier = pltpu.get_barrier_semaphore()
    partners(
        n_dp,
        dp,
        lambda p: pl.semaphore_signal(barrier, inc=1, device_id=(p, ep), device_id_type=MESH),
    )
    partners(
        n_ep,
        ep,
        lambda p: pl.semaphore_signal(barrier, inc=1, device_id=(dp, p), device_id_type=MESH),
    )

    def send_dp(stage, c, src, dst):
        def each(p):
            pltpu.make_async_remote_copy(
                src_ref=src.at[c, block_rows(p, dp_block)],
                dst_ref=dst.at[c, block_rows(dp, dp_block)],
                send_sem=send_sems.at[stage, c],
                recv_sem=recv_sems.at[stage, c],
                device_id=(p, ep),
                device_id_type=MESH,
            ).start()

        partners(n_dp, dp, each)
        dst[c, block_rows(dp, dp_block)] = src[c, block_rows(dp, dp_block)]


    def send_ep(stage, c, src, dst):
        def each(p):
            pltpu.make_async_remote_copy(
                src_ref=src.at[c, block_rows(p, ep_block)],
                dst_ref=dst.at[c, block_rows(ep, ep_block)],
                send_sem=send_sems.at[stage, c],
                recv_sem=recv_sems.at[stage, c],
                device_id=(dp, p),
                device_id_type=MESH,
            ).start()

        partners(n_ep, ep, each)
        dst[c, block_rows(ep, ep_block)] = src[c, block_rows(ep, ep_block)]

    def over_dp(stage, c):
        return (c % 2 == 0) == (stage in (0, 3))

    def hop(stage, c, src, dst):
        (send_dp if over_dp(stage, c) else send_ep)(stage, c, src, dst)

    def wait_all(sems, stage, c, ref):
        size = rows - (dp_block if over_dp(stage, c) else ep_block)
        part = ref.at[c, pl.ds(0, size)]
        pltpu.make_async_copy(part, part, sems.at[stage, c]).wait()

    def mm(a, b):
        return jnp.dot(a, b, preferred_element_type=jnp.float32)

    slot = lax.broadcasted_iota(jnp.int32, (rows, tokens), 0)
    named = jnp.zeros((rows, tokens), jnp.float32)
    weight = jnp.zeros((rows, tokens), jnp.float32)
    for k in range(TOP):
        hit = ids_ref[k : k + 1, :] == (slot >> 1)
        named += jnp.where(hit, 1.0, 0.0)
        weight += jnp.where(hit, gates_ref[k : k + 1, :], 0.0)
    first = lax.broadcasted_iota(jnp.int32, (tokens, tokens), 0)
    second = lax.broadcasted_iota(jnp.int32, (tokens, tokens), 1)
    before = jnp.where(first < second, 1.0, 0.0).astype(jnp.bfloat16)
    same = jnp.where(first == second, 1.0, 0.0).astype(jnp.bfloat16)
    chosen = mm(named.astype(jnp.bfloat16), before) == (slot & 1).astype(jnp.float32)
    pick = jnp.where(chosen, named, 0.0).astype(jnp.bfloat16)
    weight = jnp.where(chosen, weight, 0.0)
    weight_high = weight.astype(jnp.bfloat16)
    weight_low = (weight - weight_high.astype(jnp.float32)).astype(jnp.bfloat16)
    weight_high = contract_last(same, weight_high).astype(jnp.bfloat16)
    weight_low = contract_last(same, weight_low).astype(jnp.bfloat16)
    weights = jnp.concatenate([weight_high, weight_low], axis=0)
    to = lax.broadcasted_iota(jnp.int32, (rows, rows), 0)
    frm = lax.broadcasted_iota(jnp.int32, (rows, rows), 1)
    by_ep = lax.rem(to >> 1, n_dp) * dp_block + (to // ep_block) * 2 + (to & 1)
    by_dp = lax.rem(to >> 1, n_ep) * ep_block + (to // dp_block) * 2 + (to & 1)
    perm_ep = jnp.where(frm == by_ep, 1.0, 0.0).astype(jnp.bfloat16)
    perm_dp = jnp.where(frm == by_dp, 1.0, 0.0).astype(jnp.bfloat16)
    picks = (pick, mm(perm_ep, pick).astype(jnp.bfloat16))
    weights = (weights, contract_last(weights, perm_ep).astype(jnp.bfloat16))
    perms = (perm_ep, perm_dp)

    hidden = res_ref[...].astype(jnp.float32) + att_ref[...].astype(jnp.float32)
    hid[...] = hidden
    mean_square = jnp.mean(hidden * hidden, axis=1, keepdims=True)
    scale = lax.rsqrt(mean_square + norm_eps)

    pl.semaphore_wait(barrier, n_dp + n_ep - 2)

    for c in range(chunks):
        span = pl.ds(c * cols, cols)
        normed = (hid[:, span] * scale * gain_ref[span].astype(jnp.float32).reshape(1, cols)).astype(
            jnp.bfloat16
        )
        s1[c] = mm(picks[c % 2], normed).astype(jnp.bfloat16)
        hop(0, c, s1, r1)
    for c in range(chunks):
        wait_all(recv_sems, 0, c, r1)
        s2[c] = mm(perms[c % 2], r1[c]).astype(jnp.bfloat16)
        hop(1, c, s2, r2)
    loads[0].wait()
    loads[1].wait()
    for c in range(chunks):
        wait_all(recv_sems, 1, c, r2)
        span = pl.ds(c * cols, cols)
        x = r2[c]
        if c % 2:
            x = mm(perm_ep, x).astype(jnp.bfloat16)
        gate_part = mm(x, w_gate[span, :])
        up_part = mm(x, w_up[span, :])
        if c:
            gate_part += total[:, pl.ds(0, hidden_units)]
            up_part += total[:, pl.ds(hidden_units, hidden_units)]
        if c < chunks - 1:
            total[:, pl.ds(0, hidden_units)] = gate_part
            total[:, pl.ds(hidden_units, hidden_units)] = up_part
        else:
            act[0] = (gate_part / (1.0 + jnp.exp(-gate_part)) * up_part).astype(jnp.bfloat16)
    act[1] = mm(perm_dp, act[0]).astype(jnp.bfloat16)
    loads[2].wait()
    for c in range(chunks):
        o1[c] = mm(act[c % 2], w_down[:, pl.ds(c * cols, cols)]).astype(jnp.bfloat16)
        hop(2, c, o1, q1)
    for c in range(chunks):
        wait_all(recv_sems, 2, c, q1)
        q2[c] = mm(perms[1 - c % 2], q1[c]).astype(jnp.bfloat16)
        hop(3, c, q2, q3)
    for c in range(chunks):
        wait_all(recv_sems, 3, c, q3)
        span = pl.ds(c * cols, cols)
        both = mm(weights[c % 2], q3[c])
        out_ref[:, span] = hid[:, span] + (both[:tokens] + both[tokens:])
    for stage, ref in enumerate((s1, s2, o1, q2)):
        for c in range(chunks):
            wait_all(send_sems, stage, c, ref)


def moe(attention, residual, norm_gain, expert_ids, gate_weights, expert_gate, expert_up, expert_down):
    n_dp, n_ep = lax.axis_size("dp"), lax.axis_size("ep")
    tokens, width = residual.shape
    units = expert_gate.shape[2]
    rows = n_dp * n_ep * 2
    chunks = 4
    buf = pltpu.VMEM((chunks, rows, width // chunks), jnp.bfloat16)
    vmem = pl.BlockSpec(memory_space=pltpu.VMEM)
    hbm = pl.BlockSpec(memory_space=pl.ANY)
    return pl.pallas_call(
        functools.partial(moe_kernel, (n_dp, n_ep, chunks)),
        out_shape=jax.ShapeDtypeStruct((tokens, width), jnp.float32),
        in_specs=[vmem] * 5 + [hbm] * 3,
        out_specs=vmem,
        scratch_shapes=[
            pltpu.VMEM((width, units), jnp.bfloat16),
            pltpu.VMEM((width, units), jnp.bfloat16),
            pltpu.VMEM((units, width), jnp.bfloat16),
            pltpu.VMEM((tokens, width), jnp.float32),
            buf,
            buf,
            buf,
            buf,
            pltpu.VMEM((rows, 2 * units), jnp.float32),
            pltpu.VMEM((2, rows, units), jnp.bfloat16),
            buf,
            buf,
            buf,
            buf,
            pltpu.SemaphoreType.DMA((4, chunks)),
            pltpu.SemaphoreType.DMA((4, chunks)),
            pltpu.SemaphoreType.DMA((3,)),
        ],
        compiler_params=pltpu.CompilerParams(
            collective_id=1, has_side_effects=True, vmem_limit_bytes=60 * 2**20
        ),
        name="experts",
    )(
        attention,
        residual,
        norm_gain,
        expert_ids.T,
        gate_weights.T,
        expert_gate,
        expert_up,
        expert_down,
    )


def contract_last(a, b):
    return lax.dot_general(a, b, (((1,), (1,)), ((), ())), preferred_element_type=jnp.float32)


def attend(q, s_old, keys, length, positions, prefix_len, lat):
    s_new = contract_last(q, keys[prefix_len:, :])
    old_pos = lax.broadcasted_iota(jnp.int32, (1, prefix_len), 1)
    s_old = s_old + jnp.where(old_pos < length, 0.0, -1e30)
    new_pos = lax.broadcasted_iota(jnp.int32, s_new.shape, 1)
    s_new = jnp.where(new_pos <= positions, s_new, -1e30)
    top = jnp.maximum(
        jnp.max(s_old, axis=1, keepdims=True), jnp.max(s_new, axis=1, keepdims=True)
    )
    e_old = jnp.exp2((s_old - top) * exp2_scale)
    e_new = jnp.exp2((s_new - top) * exp2_scale)
    weight_sum = jnp.sum(e_old, axis=1, keepdims=True) + jnp.sum(e_new, axis=1, keepdims=True)
    weighted = jnp.dot(
        e_old.astype(jnp.bfloat16), keys[0:prefix_len, 0:lat], preferred_element_type=jnp.float32
    )
    weighted += jnp.dot(
        e_new.astype(jnp.bfloat16), keys[prefix_len:, 0:lat], preferred_element_type=jnp.float32
    )
    return (weighted * (1.0 / weight_sum)).astype(jnp.bfloat16)


SIDE = 4


def attention_kernel(
    lengths_ref,
    sources_ref,
    owner_ref,
    prefix_ref,
    new_ref,
    proj_ref,
    queries_hbm,
    value_up_hbm,
    att_ref,
    decode_ref,
    q_raw,
    value_up,
    q_home,
    q_late,
    scores,
    keys_own,
    late_own,
    late_in,
    late_on,
    rows_own,
    rows_in,
    rows_on,
    news_y,
    news_out,
    news_x,
    proj,
    heads,
    heads_late,
    part,
    part_b,
    pair,
    summed,
    gathered,
    z_recv,
    y_recv,
    dp_recv,
    x_recv,
    pair_recv,
    last_recv,
    sends,
    load_sems,
):
    dp, ep = lax.axis_index("dp"), lax.axis_index("ep")
    x, y = dp // SIDE, lax.rem(dp, SIDE)
    z, core = ep // 2, lax.rem(ep, 2)
    n_dp = SIDE * SIDE
    n_ep = 2 * SIDE
    prefix_part, new_part = prefix_ref.shape[2], new_ref.shape[1]
    prefix_len = prefix_part * n_ep
    shard_rows = prefix_part + new_part
    head_count, lat, vh = value_up.shape
    span = q_raw.shape[2]
    late = span // 4
    home = span - late
    tokens = span // n_ep
    strip = tokens // 2
    block = home // 2
    quad = head_count // 2
    col_part = proj_ref.shape[0]
    cols = col_part * SIDE
    piece = head_count * late // n_dp

    def around(a, k):
        return lax.rem(a + k + SIDE, SIDE)

    def device(x2, y2, z2, core2):
        return (x2 * SIDE + y2, z2 * 2 + core2)

    right_z, left_z = device(x, y, around(z, 1), core), device(x, y, around(z, -1), core)
    right_y, left_y = device(x, around(y, 1), z, core), device(x, around(y, -1), z, core)
    sibling = device(x, y, z, 1 - core)

    load_q = pltpu.make_async_copy(queries_hbm, q_raw, load_sems.at[0])
    load_q.start()
    load_v = pltpu.make_async_copy(value_up_hbm, value_up, load_sems.at[1])
    load_v.start()

    barrier = pltpu.get_barrier_semaphore()

    def hello(to):
        pl.semaphore_signal(barrier, inc=1, device_id=to, device_id_type=MESH)

    partners(n_dp, dp, lambda p: hello((p, ep)))
    for kz in range(1, SIDE):
        for kx in range(SIDE):
            hello(device(around(x, kx), y, around(z, kz), core))
    hello(sibling)

    def send(src, dst, to, send_sem, recv_sem):
        pltpu.make_async_remote_copy(
            src_ref=src,
            dst_ref=dst,
            send_sem=send_sem,
            recv_sem=recv_sem,
            device_id=to,
            device_id_type=MESH,
        ).start()

    def wait(sem, ref):
        pltpu.make_async_copy(ref, ref, sem).wait()

    def key_parts(buf, z2, core2, half):
        at = z2 * 2 + core2
        n, m = (prefix_part // 2, new_part // 2) if half is not None else (prefix_part, new_part)
        half = half or 0
        old = pl.multiple_of(at * prefix_part + half * n, n)
        new = pl.multiple_of(prefix_len + at * new_part + half * m, m)
        return [buf.at[pl.ds(old, n)], buf.at[pl.ds(new, m)]]

    eye_a = lax.broadcasted_iota(jnp.int32, (span, span), 0)
    eye_b = lax.broadcasted_iota(jnp.int32, (span, span), 1)
    eye = jnp.where(eye_a == eye_b, 1.0, 0.0).astype(jnp.bfloat16)
    keys_own[block_rows(ep, prefix_part)] = contract_last(eye, prefix_ref[0]).astype(jnp.bfloat16)
    keys_own[pl.ds(pl.multiple_of(prefix_len + ep * new_part, new_part), new_part)] = new_ref[0]
    proj[block_rows(y, col_part)] = proj_ref[...]

    pl.semaphore_wait(barrier, n_dp - 1 + (SIDE - 1) * SIDE + 1)

    def ring_start(refs, right, left, send_sem, recv):
        for half in (0, 1):
            for ref in refs(0, half):
                send(ref, ref, right, send_sem, recv.at[half])
            for ref in refs(0, 1 - half):
                send(ref, ref, left, send_sem, recv.at[2 + 1 - half])

    def ring_forward(refs, right, left, send_sem, recv, half_ref):
        wait(recv.at[0], half_ref)
        for ref in refs(-1, 0):
            send(ref, ref, right, send_sem, recv.at[4])
        wait(recv.at[3], half_ref)
        for ref in refs(1, 1):
            send(ref, ref, left, send_sem, recv.at[5])

    key_half = keys_own.at[pl.ds(0, shard_rows // 2)]
    key_full = keys_own.at[pl.ds(0, shard_rows)]

    def key_refs(k, half):
        return key_parts(keys_own, around(z, k), core, half)

    def share(k, sem):
        for ref in key_refs(k, None):
            send(ref, ref, sibling, sends.at[0], z_recv.at[sem])

    def everywhere(src, dst, send_sem, recv_sem):
        partners(n_dp, dp, lambda p: send(src(p), dst, (p, ep), send_sem, recv_sem))

    ring_start(key_refs, right_z, left_z, sends.at[0], z_recv)
    share(0, 6)

    def over_axis(along_x, src, dst, send_sem, recv_sem):
        for k in (2, 1, 3):
            to = device(around(x, k), y, z, core) if along_x else device(x, around(y, k), z, core)
            send(src(k), dst, to, send_sem, recv_sem)

    def proj_refs(k, half):
        n = col_part // 2
        start = pl.multiple_of(around(y, k) * col_part + half * n, n)
        return [proj.at[pl.ds(start, n)]]

    load_q.wait()
    for h in range(head_count):
        rows = contract_last(eye, q_raw[h]).astype(jnp.bfloat16)
        late_own[pl.ds(h * late, late)] = rows[home:]
        for b in range(2):
            for e in range(home // tokens):
                at = (h % quad) * block + (e % 2) * block // 2 + (e // 2) * strip
                row = e * tokens + b * strip
                q_home[2 * b + h // quad, pl.ds(at, strip)] = rows[row : row + strip]
    all_late = keys_own.at[pl.ds(0, (n_dp - 1) * piece)]
    all_rows = rows_own.at[pl.ds(0, (n_dp - 1) * piece)]
    everywhere(
        lambda p: late_own.at[block_rows(p, piece)], late_in.at[dp], sends.at[1], dp_recv.at[0]
    )
    late_in[dp] = late_own[block_rows(dp, piece)]
    all_news = keys_own.at[pl.ds(0, (SIDE - 1) * new_part)]
    news_y[y] = new_ref[0]
    over_axis(False, lambda k: news_y.at[y], news_y.at[y], sends.at[3], dp_recv.at[1])

    def score(k):
        at = pl.ds(pl.multiple_of(around(z, k) * 2 * prefix_part, 2 * prefix_part), 2 * prefix_part)

        def step(i, carry):
            scores[i, :, at] = contract_last(q_home[i], keys_own[at])
            return carry

        lax.fori_loop(0, 4, step, 0)

    wait(z_recv.at[6], key_full)
    score(0)
    ring_forward(key_refs, right_z, left_z, sends.at[0], z_recv, key_half)
    wait(z_recv.at[1], key_half)
    share(-1, 7)
    wait(z_recv.at[2], key_half)
    share(1, 8)
    wait(dp_recv.at[0], all_late)

    def stage_late(i, carry):
        slot = jnp.int32(0)
        for s in range(n_dp):
            slot = jnp.maximum(slot, jnp.where(sources_ref[s] == i, s, 0))
        late_on[i] = late_in[slot]
        return carry

    lax.fori_loop(0, n_dp, stage_late, 0)
    everywhere(
        lambda p: late_on.at[p], q_late.at[block_rows(dp, piece)], sends.at[2], dp_recv.at[2]
    )
    q_late[block_rows(dp, piece)] = late_on[dp]
    ring_start(proj_refs, right_y, left_y, sends.at[4], y_recv)
    wait(z_recv.at[7], key_full)
    score(-1)
    wait(z_recv.at[8], key_full)
    score(1)
    wait(z_recv.at[4], key_half)
    wait(z_recv.at[5], key_half)
    share(2, 9)
    load_v.wait()
    wait(z_recv.at[9], key_full)
    score(2)

    def given_to(slot):
        given = jnp.int32(0)
        for i in range(n_dp):
            given = jnp.maximum(given, jnp.where(owner_ref[i] == slot, i, 0))
        return given

    def send_heads(i, refs):
        for ref in refs:
            over_axis(True, lambda k: ref, ref, sends.at[6 + i], x_recv.at[i])

    row = lax.broadcasted_iota(jnp.int32, (quad * block, 1), 0)
    within = row
    for j in range(1, quad):
        within -= jnp.where(row >= j * block, block, 0)
    on_core = jnp.where(within >= block // 2, 1, 0)
    within -= on_core * (block // 2)
    home_pos = ((within // strip) * 2 + on_core) * tokens + lax.rem(within, strip)
    half_rows = SIDE * block // 2

    def home_part(b, half):
        positions = home_pos + b * strip
        i = 2 * b + half
        out = attend(
            q_home[i], scores[i], keys_own, lengths_ref[dp], positions, prefix_len, lat
        )
        for j in range(quad):
            h = half * quad + j
            rows = jnp.dot(
                out[j * block : (j + 1) * block], value_up[h], preferred_element_type=jnp.float32
            ).astype(jnp.bfloat16)
            for c in range(2):
                at = pl.multiple_of(c * half_rows + x * (block // 2), block // 2)
                heads[b, pl.ds(at, block // 2), pl.ds(h * vh, vh)] = rows[
                    c * block // 2 : (c + 1) * block // 2
                ]
        refs = []
        for c in range(2):
            at = pl.multiple_of(c * half_rows + x * (block // 2), block // 2)
            refs.append(
                heads.at[b, pl.ds(at, block // 2), pl.ds(half * quad * vh, quad * vh)]
            )
        send_heads(2 * b + half, refs)

    def wait_heads(i):
        wait(x_recv.at[i], heads.at[0, pl.ds(0, (SIDE - 1) * block // 2)])

    def project(i, rows):
        n = rows.shape[0]
        out = contract_last(rows, proj[...])
        part[i, pl.ds(0, n)] = out
        part_b[i, pl.ds(0, n)] = out.astype(jnp.bfloat16)
        other = part_b.at[i, pl.ds(pl.multiple_of((1 - core) * (n // 2), n // 2), n // 2)]
        send(other, pair.at[i, pl.ds(0, n // 2)], sibling, sends.at[11 + i], pair_recv.at[i])

    def pass_on(i, n, to_z, size, offset):
        wait(pair_recv.at[i], pair.at[i, pl.ds(0, n // 2)])
        mine = part[i, pl.ds(pl.multiple_of(core * (n // 2), n // 2), n // 2)]
        both = mine + pair[i, pl.ds(0, n // 2)].astype(jnp.float32)
        summed[i, pl.ds(0, n // 2)] = both.astype(jnp.bfloat16)
        start = (x * SIDE + z) * tokens + offset
        landing = pl.ds(pl.multiple_of(start, size), size)
        for k in (2, 1, 3, 0):
            xk = around(x, k)
            for j, zk in enumerate(to_z):
                at = pl.multiple_of((xk * len(to_z) + j) * size, size)

                def go():
                    send(
                        summed.at[i, pl.ds(at, size)],
                        gathered.at[landing],
                        device(xk, y, zk, core),
                        sends.at[14],
                        last_recv,
                    )

                if k:
                    go()
                else:
                    pl.when(z != zk)(go)

                    @pl.when(z == zk)
                    def _():
                        gathered[landing] = summed[i, pl.ds(at, size)]

    home_part(0, 0)
    wait(dp_recv.at[1], all_news)
    for k in range(SIDE):
        slot = around(x, k) * SIDE + y
        news_out[k] = news_y[lax.rem(given_to(slot), SIDE)]
    over_axis(True, lambda k: news_out.at[k], news_x.at[x], sends.at[15], dp_recv.at[5])
    news_x[x] = news_out[0]
    home_part(0, 1)
    proj_half = proj.at[pl.ds(0, col_part // 2)]
    ring_forward(proj_refs, right_y, left_y, sends.at[4], y_recv, proj_half)
    wait(dp_recv.at[2], all_late)
    late_row = lax.broadcasted_iota(jnp.int32, (head_count * late, 1), 0)
    late_pos = lax.rem(late_row, late) + home
    late_scores = contract_last(q_late[...], keys_own[0:prefix_len, :])
    out = attend(
        q_late[...], late_scores, keys_own, lengths_ref[dp], late_pos, prefix_len, lat
    )
    for h in range(head_count):
        rows_own[pl.ds(h * late, late)] = jnp.dot(
            out[h * late : (h + 1) * late], value_up[h], preferred_element_type=jnp.float32
        ).astype(jnp.bfloat16)
    everywhere(
        lambda p: rows_own.at[block_rows(p, piece)], rows_in.at[dp], sends.at[5], dp_recv.at[3]
    )
    rows_in[dp] = rows_own[block_rows(dp, piece)]
    home_part(1, 0)
    wait(dp_recv.at[3], all_rows)

    def stage_rows(s, carry):
        at = pl.multiple_of((s // SIDE) * piece, piece)
        rows_on[lax.rem(s, SIDE), pl.ds(at, piece)] = rows_in[sources_ref[s]]
        return carry

    lax.fori_loop(0, n_dp, stage_rows, 0)
    quarter = SIDE * piece
    landing = (
        pl.ds(pl.multiple_of(lax.rem(dp, 2) * quarter, quarter), quarter),
        pl.ds(pl.multiple_of((dp // 2) * vh, vh), vh),
    )
    everywhere(
        lambda p: rows_on.at[lax.rem(p, SIDE)],
        heads_late.at[landing],
        sends.at[16],
        dp_recv.at[4],
    )
    heads_late[landing] = rows_on[y]
    all_late_heads = heads_late.at[pl.ds(0, (n_dp - 1) * quarter * vh // heads_late.shape[1])]
    for i in (1, 2, 4, 5):
        wait(y_recv.at[i], proj_half)
    wait_heads(0)
    wait_heads(1)
    project(0, heads[0])
    home_z = tuple(range(home // tokens // 2))
    late_z = (SIDE - 1,)
    home_rows, late_rows = SIDE * block, SIDE * late
    pass_on(0, home_rows, home_z, strip, 0)
    home_part(1, 1)
    wait(dp_recv.at[4], all_late_heads)
    project(2, heads_late[...])
    pass_on(2, late_rows, late_z, tokens, 0)
    wait_heads(2)
    wait_heads(3)
    project(1, heads[1])
    pass_on(1, home_rows, home_z, strip, strip)
    wait(dp_recv.at[5], all_news)
    decode_ref[0] = news_x[given_to(dp) // SIDE]
    wait(last_recv, gathered.at[pl.ds(0, (n_dp - 1) * tokens)])
    for k in range(SIDE):
        total = gathered[pl.ds(k * SIDE * tokens, tokens)].astype(jnp.float32)
        for j in range(1, SIDE):
            total += gathered[pl.ds((k * SIDE + j) * tokens, tokens)].astype(jnp.float32)
        att_ref[:, pl.ds(k * cols, cols)] = total

    wait(sends.at[0], keys_own.at[pl.ds(0, 3 * shard_rows + 4 * shard_rows)])
    wait(sends.at[1], all_late)
    wait(sends.at[2], all_late)
    wait(sends.at[3], all_news)
    wait(sends.at[15], all_news)
    wait(sends.at[4], proj.at[pl.ds(0, 3 * col_part)])
    wait(sends.at[5], all_rows)
    wait(sends.at[16], all_late_heads)
    for i in range(4):
        wait(sends.at[6 + i], heads.at[0, pl.ds(0, (SIDE - 1) * block // 2)])
    for i in range(2):
        wait(sends.at[11 + i], pair.at[i])
    wait(sends.at[13], pair.at[2, pl.ds(0, late_rows // 2)])
    wait(sends.at[14], gathered.at[pl.ds(0, (n_dp - 1) * tokens)])


def attention(queries, prefix_latents, new_latents, lengths, sources, value_up, out_proj, owner):
    span, head_count, key_width = queries.shape
    _, lat, vh = value_up.shape
    n_dp, n_ep = lax.axis_size("dp"), lax.axis_size("ep")
    late = span // 4
    home = span - late
    late_rows = head_count * late
    prefix_part, new_part = prefix_latents.shape[1], new_latents.shape[1]
    key_rows = (prefix_part + new_part) * n_ep
    rows, col_part = out_proj.shape
    cols = col_part * SIDE
    tokens = span // n_ep
    vmem = pl.BlockSpec(memory_space=pltpu.VMEM)
    smem = pl.BlockSpec(memory_space=pltpu.SMEM)
    hbm = pl.BlockSpec(memory_space=pl.ANY)
    bf16, f32 = jnp.bfloat16, jnp.float32
    return pl.pallas_call(
        attention_kernel,
        out_shape=(
            jax.ShapeDtypeStruct((tokens, cols * SIDE), f32),
            jax.ShapeDtypeStruct(new_latents.shape, bf16),
        ),
        in_specs=[smem] * 3 + [vmem] * 3 + [hbm] * 2,
        out_specs=(vmem, vmem),
        scratch_shapes=[
            pltpu.VMEM((head_count, key_width, span), bf16),
            pltpu.VMEM(value_up.shape, bf16),
            pltpu.VMEM((4, head_count // 2 * (home // 2), key_width), bf16),
            pltpu.VMEM((late_rows, key_width), bf16),
            pltpu.VMEM((4, head_count // 2 * (home // 2), prefix_part * n_ep), f32),
            pltpu.VMEM((key_rows, key_width), bf16),
            pltpu.VMEM((late_rows, key_width), bf16),
            pltpu.VMEM((n_dp, late_rows // n_dp, key_width), bf16),
            pltpu.VMEM((n_dp, late_rows // n_dp, key_width), bf16),
            pltpu.VMEM((late_rows, vh), bf16),
            pltpu.VMEM((n_dp, late_rows // n_dp, vh), bf16),
            pltpu.VMEM((SIDE, SIDE * late_rows // n_dp, vh), bf16),
            pltpu.VMEM((SIDE, new_part, key_width), bf16),
            pltpu.VMEM((SIDE, new_part, key_width), bf16),
            pltpu.VMEM((SIDE, new_part, key_width), bf16),
            pltpu.VMEM((cols, rows), bf16),
            pltpu.VMEM((2, SIDE * home // 2, rows), bf16),
            pltpu.VMEM((SIDE * late, rows), bf16),
            pltpu.VMEM((3, SIDE * home // 2, cols), f32),
            pltpu.VMEM((3, SIDE * home // 2, cols), bf16),
            pltpu.VMEM((3, SIDE * home // 4, cols), bf16),
            pltpu.VMEM((3, SIDE * home // 4, cols), bf16),
            pltpu.VMEM((n_dp * tokens, cols), bf16),
            pltpu.SemaphoreType.DMA((10,)),
            pltpu.SemaphoreType.DMA((6,)),
            pltpu.SemaphoreType.DMA((6,)),
            pltpu.SemaphoreType.DMA((5,)),
            pltpu.SemaphoreType.DMA((3,)),
            pltpu.SemaphoreType.DMA,
            pltpu.SemaphoreType.DMA((17,)),
            pltpu.SemaphoreType.DMA((2,)),
        ],
        compiler_params=pltpu.CompilerParams(
            collective_id=2, has_side_effects=True, vmem_limit_bytes=60 * 2**20
        ),
        name="attention",
    )(
        lengths,
        sources,
        owner,
        prefix_latents.transpose(0, 2, 1),
        new_latents,
        out_proj.T,
        queries.transpose(1, 2, 0),
        value_up,
    )


def shards(
    queries,
    prefix_latents,
    new_latents,
    prefix_lengths,
    span_sources,
    value_up,
    out_proj,
    residual,
    norm_gain,
    expert_gate,
    expert_up,
    expert_down,
    expert_ids,
    gate_weights,
    decode_owner,
):
    attention_sum, decode_latents = attention(
        queries,
        prefix_latents,
        new_latents,
        prefix_lengths,
        span_sources,
        value_up,
        out_proj,
        decode_owner,
    )
    layer_out = moe(
        attention_sum,
        residual,
        norm_gain,
        expert_ids,
        gate_weights,
        expert_gate,
        expert_up,
        expert_down,
    ).astype(jnp.bfloat16)
    return (layer_out, decode_latents)


def solution(mesh):
    return jax.shard_map(
        shards,
        mesh=mesh,
        in_specs=(
            P("dp", "ep", None),
            P("dp", "ep", None),
            P("dp", "ep", None),
            P(),
            P(),
            P("ep", None, None),
            P("ep", "dp"),
            P(("dp", "ep"), None),
            P(),
            P(("dp", "ep"), None, None),
            P(("dp", "ep"), None, None),
            P(("dp", "ep"), None, None),
            P(("dp", "ep"), None),
            P(("dp", "ep"), None),
            P(),
        ),
        out_specs=(P(("dp", "ep"), None), P("dp", "ep", None)),
        check_vma=False,
    )
```
